128 devices in a mesh: fsdp: 4 (over x), sp: 16 (over z, y_lo, core), blk: 2 (over y_hi).
Axes of the slice: x: 4, y: 4 (y_hi: 2, y_lo: 2; y = y_hi * 2 + y_lo), z: 4, core: 2. Of those that a mesh axis runs over, the one named last changes fastest.
Arguments:
- tokens: bfloat16 [16384, 1024], P(('fsdp', 'sp', 'blk')), may hold values from -6 to 6
- w_qkv: bfloat16 [1024, 3072], P('fsdp'), may hold values from -0.1875 to 0.1875
- bias_q: bfloat16 [1024], P('fsdp'), may hold values from -3 to 3
- bias_v: bfloat16 [1024], P('fsdp'), may hold values from -0.119628906 to 0.119628906
- w_out: bfloat16 [1024, 1024], P('fsdp'), may hold values from -4 to 4
- bias_o: bfloat16 [1024], P('fsdp'), may hold values from -2 to 2
- gain_attn: bfloat16 [1024], P('fsdp'), may hold values from 0.5 to 1.5
- shift_attn: bfloat16 [1024], P('fsdp'), may hold values from -2 to 2
- w_in: bfloat16 [1024, 4096], P('fsdp'), may hold values from -0.1875 to 0.1875
- bias_in: bfloat16 [4096], P('fsdp'), may hold values from -2 to 2
- w_fin: bfloat16 [4096, 1024], P('fsdp'), may hold values from -0.09375 to 0.09375
- bias_fin: bfloat16 [1024], P('fsdp'), may hold values from -2 to 2
- gain_ffn: bfloat16 [1024], P('fsdp'), may hold values from 0.5 to 1.5
- shift_ffn: bfloat16 [1024], P('fsdp'), may hold values from -2 to 2
- cotangent: bfloat16 [16384, 1024], P(('fsdp', 'sp', 'blk')), may hold values from -6 to 6
Outputs:
- layer_out: bfloat16 [16384, 1024], P(('fsdp', 'sp', 'blk'))
- grad_tokens: float32 [16384, 1024], P(('fsdp', 'sp', 'blk'))
- grad_w_qkv: float32 [1024, 3072], P('fsdp')
- grad_bias_q: float32 [1024], P('fsdp')
- grad_bias_v: float32 [1024], P('fsdp')
- grad_w_out: float32 [1024, 1024], P('fsdp')
- grad_bias_o: float32 [1024], P('fsdp')
- grad_gain_attn: float32 [1024], P('fsdp')
- grad_shift_attn: float32 [1024], P('fsdp')
- grad_w_in: float32 [1024, 4096], P('fsdp')
- grad_bias_in: float32 [4096], P('fsdp')
- grad_w_fin: float32 [4096, 1024], P('fsdp')
- grad_bias_fin: float32 [1024], P('fsdp')
- grad_gain_ffn: float32 [1024], P('fsdp')
- grad_shift_ffn: float32 [1024], P('fsdp')
The draws below stay inside these ranges and needn't reach their ends.
All inputs are finite; a program needn't handle non-finite values.
Results may differ from the reference program's by a relative error of at most 0.03.
Values may be sent and summed in bfloat16 or wider, within the bound.
No kernel may reach another device: no remote copies, remote signals or barrier semaphores. Data moves between devices by JAX's collectives and lax.ppermute only.
A program may use at most 128 MiB of HBM per device.

```python
import math
import jax
import jax.numpy as jnp
from jax import lax

D = 1024
FF = 4096
HEADS = 16
HEAD_DIM = 64
LEN = 2048
TOKENS = 16384


def levels(own_key, shape, pieces, least, top_value):
    loudness = 1.0
    for position, blocks in pieces:
        heights = jax.random.uniform(jax.random.fold_in(jax.random.fold_in(own_key, 6), position), (blocks,), jnp.float32, least / len(pieces), top_value / len(pieces))
        loudness = loudness * jnp.repeat(jnp.exp(heights), shape[position] // blocks).reshape((-1,) + (1,) * (len(shape) - 1 - position))
    return loudness


def scatter_about(stream_key, extent, width, bound, pieces=(), kind=jnp.bfloat16):
    array = width * jax.random.normal(stream_key, extent, jnp.float32)
    if pieces:
        array = array * levels(stream_key, extent, pieces, -0.22, 0.18)
    return jnp.clip(array, -bound, bound).astype(kind)


def setup_inputs(seed: int = 0) -> dict:
    splits = jax.random.split(jax.random.key(seed), 16)
    tokens = scatter_about(splits[0], (TOKENS, D), 1.0, 6.0, ((0, 128),))
    w_qkv = scatter_about(splits[1], (D, 3 * D), D ** -0.5, 0.1875, ((0, 4),))
    bias_q = scatter_about(splits[2], (D,), 0.5, 3.0, ((0, 4),))
    bias_v = scatter_about(splits[3], (D,), 0.02, 0.119628906, ((0, 4),))
    w_out = scatter_about(splits[4], (D, D), (max(1, 4 * D // LEN)) ** -0.5, 4.0, ((0, 4),))
    bias_o = scatter_about(splits[5], (D,), 0.3, 2.0, ((0, 4),))
    gain_attn = jnp.clip(1.0 + 0.1 * jax.random.normal(splits[6], (D,), jnp.float32), 0.5, 1.5).astype(jnp.bfloat16)
    shift_attn = scatter_about(splits[7], (D,), 0.3, 2.0, ((0, 4),))
    w_in = scatter_about(splits[8], (D, FF), D ** -0.5, 0.1875, ((0, 4),))
    bias_in = scatter_about(splits[9], (FF,), 0.3, 2.0, ((0, 4),))
    w_fin = scatter_about(splits[10], (FF, D), FF ** -0.5, 0.09375, ((0, 4),))
    bias_fin = scatter_about(splits[11], (D,), 0.3, 2.0, ((0, 4),))
    gain_ffn = jnp.clip(1.0 + 0.1 * jax.random.normal(splits[12], (D,), jnp.float32), 0.5, 1.5).astype(jnp.bfloat16)
    shift_ffn = scatter_about(splits[13], (D,), 0.3, 2.0, ((0, 4),))
    cotangent = scatter_about(splits[14], (TOKENS, D), 1.0, 6.0, ((0, 128),))
    return dict(tokens=tokens, w_qkv=w_qkv, bias_q=bias_q, bias_v=bias_v, w_out=w_out, bias_o=bias_o, gain_attn=gain_attn, shift_attn=shift_attn, w_in=w_in, bias_in=bias_in, w_fin=w_fin, bias_fin=bias_fin, gain_ffn=gain_ffn, shift_ffn=shift_ffn, cotangent=cotangent)


@jax.custom_vjp
def low(v):
    return lax.optimization_barrier(v.astype(jnp.bfloat16)).astype(jnp.float32)

@jax.custom_vjp
def low_back(v):
    return v

def low_keep(v):
    return (low(v), None)

def low_pass(kept, grad):
    return (grad,)

def back_keep(v):
    return (v, None)

def back_low(kept, grad):
    return (low(grad),)
low.defvjp(low_keep, low_pass)
low_back.defvjp(back_keep, back_low)
norm_eps = 1e-12

def product(left_op, right_op):
    return jnp.dot(left_op, right_op, precision=lax.Precision.HIGHEST, preferred_element_type=jnp.float32)

def layer_norm(summed, gain, shift):
    row_mean = lax.optimization_barrier(jnp.mean(summed, -1, keepdims=True))
    centered = summed - row_mean
    spread = lax.optimization_barrier(jnp.mean(centered * centered, -1, keepdims=True))
    return centered * lax.rsqrt(spread + norm_eps) * gain + shift

def attention(queries, key_rows, values):
    seq_len = queries.shape[0]
    block_rows = min(512, seq_len)
    scale = 1.0 / math.sqrt(HEAD_DIM)
    query_blocks = queries.reshape(seq_len // block_rows, block_rows, HEADS, HEAD_DIM)

    def one_block(query_block):
        scores = jnp.einsum('qhd,khd->hqk', query_block, key_rows, precision=lax.Precision.HIGHEST, preferred_element_type=jnp.float32) * scale
        scores = low_back(scores)
        top_score = lax.optimization_barrier(jnp.max(scores, -1, keepdims=True))
        weights = jnp.exp(scores - top_score)
        weights = weights / lax.optimization_barrier(jnp.sum(weights, -1, keepdims=True))
        return jnp.einsum('hqk,khd->qhd', low(weights), values, precision=lax.Precision.HIGHEST, preferred_element_type=jnp.float32)
    return lax.map(jax.checkpoint(one_block), query_blocks).reshape(seq_len, HEADS * HEAD_DIM)

def forward(seq_tokens, w_qkv, bias_q, bias_v, w_out, bias_o, gain_attn, shift_attn, w_in, bias_in, w_fin, bias_fin, gain_ffn, shift_ffn):
    model_width = seq_tokens.shape[1]
    seq_len = seq_tokens.shape[0]
    head_shape = (seq_len, HEADS, HEAD_DIM)
    projected = product(seq_tokens, w_qkv)
    queries = low(low_back(projected[:, :model_width] + bias_q))
    key_rows = low(low_back(projected[:, model_width:2 * model_width]))
    values = low(low_back(projected[:, 2 * model_width:] + bias_v))
    attended = attention(queries.reshape(head_shape), key_rows.reshape(head_shape), values.reshape(head_shape))
    attended = low(low_back(attended))
    branch = low_back(product(attended, w_out) + bias_o)
    first_norm = layer_norm(seq_tokens + branch, gain_attn, shift_attn)
    pre_act = low_back(product(low(first_norm), w_in) + bias_in)
    activated = low(jax.nn.gelu(pre_act, approximate=False))
    ffn_out = low_back(product(activated, w_fin) + bias_fin)
    return layer_norm(first_norm + ffn_out, gain_ffn, shift_ffn)

def reference(tokens, w_qkv, bias_q, bias_v, w_out, bias_o, gain_attn, shift_attn, w_in, bias_in, w_fin, bias_fin, gain_ffn, shift_ffn, cotangent):
    params = tuple((weight.astype(jnp.float32) for weight in (w_qkv, bias_q, bias_v, w_out, bias_o, gain_attn, shift_attn, w_in, bias_in, w_fin, bias_fin, gain_ffn, shift_ffn)))
    model_width = tokens.shape[1]
    seq_count = tokens.shape[0] // LEN
    seq_inputs = tokens.astype(jnp.float32).reshape(seq_count, LEN, model_width)
    seq_cotan = cotangent.astype(jnp.float32).reshape(seq_count, LEN, model_width)

    def one_sequence(running, seq_item):
        seq_tokens, seq_grad = seq_item
        seq_out, pull_back = jax.vjp(forward, seq_tokens, *params)
        gradients = pull_back(seq_grad)
        running = tuple((total + part for total, part in zip(running, gradients[1:])))
        return (running, (seq_out.astype(jnp.bfloat16), gradients[0]))
    zero_grads = tuple((jnp.zeros_like(weight) for weight in params))
    totals, (seq_outs, seq_grads) = lax.scan(one_sequence, zero_grads, (seq_inputs, seq_cotan))
    layer_out = seq_outs.reshape(seq_count * LEN, model_width)
    grad_tokens = seq_grads.reshape(seq_count * LEN, model_width)
    return (layer_out, grad_tokens, totals[0], totals[1], totals[2], totals[3], totals[4], totals[5], totals[6], totals[7], totals[8], totals[9], totals[10], totals[11], totals[12])
```

```python
import functools
import math

import jax
import jax.numpy as jnp
from jax import lax
from jax.experimental import pallas as pl
from jax.experimental.pallas import tpu as pltpu
from jax.sharding import Mesh, PartitionSpec as P

AXES = ("x", "zh", "zl", "yl", "c", "yh")
SIZES = (4, 2, 2, 2, 2, 2)
SEQ_AXES = ("zl", "yl", "c", "yh")
Y_AXES = ("yl", "yh")
Z_AXES = ("zh", "zl")
D = 1024
FF = 4096
HEAD_DIM = 64
F32 = jnp.float32
BF16 = jnp.bfloat16

norm_eps = 1e-12
inv_root_two = 1.0 / math.sqrt(2.0)
inv_root_tau = 1.0 / math.sqrt(2.0 * math.pi)


def y_slot(y):
    return (y % 2) * 2 + y // 2


def shift(value, axis, step):
    slot = y_slot if axis == Y_AXES else (lambda i: i)
    return lax.ppermute(value, axis, [(slot(i), slot((i + step) % 4)) for i in range(4)])


def swap(value, axis):
    return lax.ppermute(value, axis, [(0, 1), (1, 0)])


def fetch_all(value, axis):
    return [value] + [shift(value, axis, -j) for j in (1, 2, 3)]


def scatter_sum(block_of, axis, me):
    total = block_of(me).astype(F32)
    for j in (2, 1, 3):
        total = total + shift(block_of((me + j) % 4).astype(BF16), axis, j).astype(F32)
    return total


def roll_blocks(blocks, me):
    twice = jnp.stack(blocks + blocks)
    return lax.dynamic_slice_in_dim(twice, (4 - me) % 4, 4, 0)


def dot(left_op, right_op):
    return jnp.dot(left_op, right_op, preferred_element_type=F32)


def outer_sum(left_op, right_op):
    return lax.dot_general(left_op, right_op, (((0,), (0,)), ((), ())), preferred_element_type=F32)


def times_trans(left_op, right_op):
    return lax.dot_general(left_op, right_op, (((1,), (1,)), ((), ())), preferred_element_type=F32)


def norm_parts(summed):
    row_mean = jnp.mean(summed, -1, keepdims=True)
    centered = summed - row_mean
    factor = lax.rsqrt(jnp.mean(centered * centered, -1, keepdims=True) + norm_eps)
    return (centered * factor, factor)


def norm_back(scaled_grad, normed, factor):
    return factor * (
        scaled_grad
        - jnp.mean(scaled_grad, -1, keepdims=True)
        - normed * jnp.mean(scaled_grad * normed, -1, keepdims=True)
    )


def gelu_slope(pre_act):
    return (
        0.5 * (1.0 + lax.erf(pre_act * inv_root_two))
        + pre_act * jnp.exp(-0.5 * pre_act * pre_act) * inv_root_tau
    )


def column_sum(values):
    return jnp.sum(values.astype(F32), 0)


def three_terms(column):
    high = column.astype(BF16).astype(F32)
    rest = column - high
    middle = rest.astype(BF16).astype(F32)
    return high, middle, rest - middle


def widen(values, column):
    rows = values.shape[0]
    lane = lax.broadcasted_iota(jnp.int32, (rows, HEAD_DIM), 1)
    high, middle, low = three_terms(-column)
    extra = jnp.where(lane == 0, high, jnp.where(lane == 1, middle, jnp.where(lane == 2, low, 0.0)))
    return jnp.concatenate([values.astype(F32), extra], 1).astype(BF16)


def with_ones(values):
    rows = values.shape[0]
    lane = lax.broadcasted_iota(jnp.int32, (rows, HEAD_DIM), 1)
    return jnp.concatenate([values.astype(F32), jnp.where(lane < 3, 1.0, 0.0)], 1).astype(BF16)


def attend_kernel(place, *refs):
    pieces = refs[:8]
    weight, bias, q_out, k_out, v_out, attf_out, att_out = refs[8:]
    for i in range(8):
        proj = dot(pieces[i][...], weight[...]) + bias[...]
        rows = pl.ds(256 * i, 256)
        query = proj[:, :64].astype(BF16).astype(F32) * 0.125
        q_out[rows, :] = jnp.concatenate([query, jnp.zeros_like(query)], 1).astype(BF16)
        k_out[rows, :] = with_ones(proj[:, 64:128])
        v_out[rows, :] = with_ones(proj[:, 128:192])

    @pl.loop(0, 8)
    def _(i):
        rows = pl.ds(pl.multiple_of(256 * i, 256), 256)
        query = q_out[rows, :]
        scores = times_trans(query, k_out[...])
        top = jnp.max(scores, 1, keepdims=True)
        probs = jnp.exp(scores - top).astype(BF16)
        weighted = dot(probs, v_out[...])
        total = weighted[:, 64:65]
        attended = weighted[:, :64] / total
        q_out[rows, :] = widen(query[:, :64], top + jnp.log(total))
        attf_out[rows, :] = attended
        att_out[place[2 * i]] = attended[:128].astype(BF16)
        att_out[place[2 * i + 1]] = attended[128:].astype(BF16)


def attend(place, pieces, weight, bias):
    vmem = pl.BlockSpec(memory_space=pltpu.VMEM)
    wide = jax.ShapeDtypeStruct((2048, 128), BF16)
    return pl.pallas_call(
        attend_kernel,
        in_specs=[pl.BlockSpec(memory_space=pltpu.SMEM)] + [vmem] * 10,
        out_specs=[vmem] * 5,
        out_shape=[
            wide,
            wide,
            wide,
            jax.ShapeDtypeStruct((2048, 64), F32),
            jax.ShapeDtypeStruct((16, 128, 64), BF16),
        ],
        compiler_params=pltpu.CompilerParams(vmem_limit_bytes=48 * 2**20),
        cost_estimate=pl.CostEstimate(flops=3 * 10**9, bytes_accessed=6 * 10**6, transcendentals=2**22),
        name="attend",
    )(place, *pieces, weight, bias)


def attend_back_kernel(place, q_ref, k_ref, v_ref, attf, dout, rel_out, abs_out, g_wide, dq_acc):
    for r in range(16):
        rows = pl.ds(128 * r, 128)
        grad = dout[place[r]]
        delta = jnp.sum(grad.astype(F32) * attf[rows, :], 1, keepdims=True)
        g_wide[rows, :] = widen(grad, delta)
    dq_acc[...] = jnp.zeros_like(dq_acc)

    @pl.loop(0, 8)
    def _(j):
        rows = pl.ds(pl.multiple_of(256 * j, 256), 256)
        keys = k_ref[rows, :]
        probs = jnp.exp(times_trans(keys, q_ref[...]))
        d_less = times_trans(v_ref[rows, :], g_wide[...])
        d_scores = (probs * d_less).astype(BF16)
        d_val = dot(probs.astype(BF16), g_wide[...])[:, :64]
        d_key = dot(d_scores, q_ref[...])[:, :64]
        dq_acc[...] += outer_sum(d_scores, keys)
        both = jnp.concatenate([jnp.zeros_like(d_key), d_key, d_val], 1).astype(BF16)
        rel_out[rows, :] = both

    for r in range(16):
        rows = pl.ds(128 * r, 128)
        d_query = (dq_acc[rows, :][:, :64] * 0.125).astype(BF16)
        both = jnp.concatenate([d_query, rel_out[rows, :][:, 64:192]], 1)
        rel_out[rows, :] = both
        abs_out[place[r]] = both


def attend_back(place, q_wide, k_wide, v_wide, attf, dout):
    vmem = pl.BlockSpec(memory_space=pltpu.VMEM)
    return pl.pallas_call(
        attend_back_kernel,
        in_specs=[pl.BlockSpec(memory_space=pltpu.SMEM)] + [vmem] * 5,
        out_specs=[vmem] * 2,
        out_shape=[
            jax.ShapeDtypeStruct((2048, 192), BF16),
            jax.ShapeDtypeStruct((16, 128, 192), BF16),
        ],
        scratch_shapes=[pltpu.VMEM((2048, 128), BF16), pltpu.VMEM((2048, 128), F32)],
        compiler_params=pltpu.CompilerParams(vmem_limit_bytes=48 * 2**20),
        cost_estimate=pl.CostEstimate(flops=10**10, bytes_accessed=4 * 10**6, transcendentals=2**22),
        name="attend_back",
    )(place, q_wide, k_wide, v_wide, attf, dout)


def lay_ffn_kernel(where, *refs):
    grads = refs[:8]
    win_out, wfin_out, wout_out, vec_out = refs[8:]
    x, y, z, c = where[0], where[1], where[2], where[3]
    for cj in range(2):
        core = (c + cj) % 2
        for yj in range(4):
            for zj in range(4):
                chip = ((y + yj) % 4) * 4 + (z + zj) % 4
                piece = grads[cj * 4 + yj]
                for xj in range(4):
                    owner = (x + 4 - xj) % 4
                    col = pl.multiple_of(owner * 1024 + core * 512, 512)
                    win_out[pl.ds(pl.multiple_of(chip * 16, 16), 16), pl.ds(col, 512)] = piece[
                        zj, 16 * xj : 16 * xj + 16
                    ].astype(F32)
                for half in range(2):
                    wfin_out[
                        pl.ds(pl.multiple_of(core * 512 + chip * 32, 32), 32),
                        512 * half : 512 * half + 512,
                    ] = piece[zj, 64 + 32 * half : 96 + 32 * half].astype(F32)
                rest = piece[zj, 128:160].astype(F32)
                for half in range(2):
                    wout_out[
                        pl.ds(pl.multiple_of(core * 128 + chip * 8, 8), 8),
                        512 * half : 512 * half + 512,
                    ] = rest[8 * half : 8 * half + 8]
                vec_out[core * 16 + chip] = rest[16:24, 0:128]


def lay_qkv_kernel(where, *refs):
    grads = refs[:8]
    w_out, b_out = refs[8:]
    y, z, c = where[1], where[2], where[3]
    for cj in range(2):
        core = (c + cj) % 2
        for yj in range(2):
            y_now = (y + yj) % 4
            swapped = y_now // 2 == 1
            for zj in range(4):
                z_now = (z + zj) % 4
                first = grads[cj * 4 + yj][zj].astype(F32)
                second = grads[cj * 4 + yj + 2][zj].astype(F32)
                low = jnp.where(swapped, second, first)
                high = jnp.where(swapped, first, second)
                head = (z_now % 2) * 8 + (y_now % 2) * 4 + core * 2
                for part in range(3):
                    lanes = slice(part * 64, part * 64 + 64)
                    pair = jnp.concatenate([low[:, lanes], high[:, lanes]], 1)
                    col = pl.multiple_of(part * 1024 + head * 64, 128)
                    w_out[
                        pl.ds(pl.multiple_of((z_now // 2) * 128, 128), 128), pl.ds(col, 128)
                    ] = pair[:128]
                    b_out[:, pl.ds(col, 128)] = pair[128:136]


def lay(kernel, where, grads, shapes, name):
    vmem = pl.BlockSpec(memory_space=pltpu.VMEM)
    return pl.pallas_call(
        kernel,
        in_specs=[pl.BlockSpec(memory_space=pltpu.SMEM)] + [vmem] * len(grads),
        out_specs=[vmem] * len(shapes),
        out_shape=[jax.ShapeDtypeStruct(s, F32) for s in shapes],
        compiler_params=pltpu.CompilerParams(vmem_limit_bytes=48 * 2**20),
        cost_estimate=pl.CostEstimate(flops=10**6, bytes_accessed=15 * 10**6, transcendentals=0),
        name=name,
    )(where, *grads)


def shards(
    tokens,
    w_qkv,
    bias_q,
    bias_v,
    w_out,
    bias_o,
    gain_attn,
    shift_attn,
    w_in,
    bias_in,
    w_fin,
    bias_fin,
    gain_ffn,
    shift_ffn,
    cotangent,
):
    x = lax.axis_index("x")
    zh = lax.axis_index("zh")
    zl = lax.axis_index("zl")
    yl = lax.axis_index("yl")
    c = lax.axis_index("c")
    yh = lax.axis_index("yh")
    y = yh * 2 + yl
    z = zh * 2 + zl
    head = zl * 8 + yl * 4 + c * 2 + yh
    where = jnp.stack([x, y, z, c]).astype(jnp.int32)
    places = []
    for cj in range(2):
        for yj in range(4):
            for zj in range(2):
                y_now = (y + yj) % 4
                places.append(((zl + zj) % 2) * 8 + (y_now % 2) * 4 + ((c + cj) % 2) * 2 + y_now // 2)
    place = jnp.stack(places).astype(jnp.int32)

    head_cols = lax.dynamic_slice(w_qkv.reshape(256, 3, 1024), (0, 0, head * 64), (256, 3, 64))
    head_blocks = fetch_all(head_cols.reshape(256, 192), "x")
    pair = jnp.concatenate([tokens, swap(tokens, "zl")], 0)
    mine = fetch_all(pair, Y_AXES)
    pieces = mine + [swap(part, "c") for part in mine]
    vectors = jnp.stack(
        [bias_q, bias_v, bias_o, gain_attn, shift_attn, bias_fin, gain_ffn, shift_ffn]
    )
    full = roll_blocks(fetch_all(vectors, "x"), x).transpose(1, 0, 2).reshape(8, 1024).astype(F32)
    full_bq, full_bv, full_bo, full_g1, full_s1, full_bf, full_g2, full_s2 = [
        full[i] for i in range(8)
    ]
    weight_out = lax.all_gather(w_out, "x", axis=0, tiled=True)
    weight_qkv = lax.all_gather(w_qkv, "x", axis=0, tiled=True)

    in_blocks = []
    for j in range(4):
        part = lax.dynamic_slice(w_in, (0, ((x + j) % 4) * 1024 + c * 512), (256, 512))
        in_blocks.append(part if j == 0 else shift(part, "x", j))
    in_blocks = [in_blocks[0], in_blocks[3], in_blocks[2], in_blocks[1]]
    in_slice = roll_blocks(in_blocks, x).reshape(1024, 512)
    fin_slice = lax.dynamic_slice(w_fin, (c * 512, 0), (512, 1024))
    bias_slice = lax.dynamic_slice(bias_in, (c * 512,), (512,)).astype(F32)

    weight_head = roll_blocks(head_blocks, x).reshape(1024, 192)
    bias_head = jnp.concatenate(
        [
            lax.dynamic_slice(full_bq, (head * 64,), (64,)),
            jnp.zeros((64,), F32),
            lax.dynamic_slice(full_bv, (head * 64,), (64,)),
        ]
    ).reshape(1, 192)
    q_wide, k_wide, v_wide, attf, att_blocks = attend(place, pieces, weight_head, bias_head)
    attended = (
        lax.all_to_all(att_blocks, SEQ_AXES, split_axis=0, concat_axis=0, tiled=True)
        .transpose(1, 0, 2)
        .reshape(128, 1024)
    )

    first_sum = tokens.astype(F32) + dot(attended, weight_out) + full_bo
    normed_one, factor_one = norm_parts(first_sum)
    first_norm = normed_one * full_g1 + full_s1
    norm_low = first_norm.astype(BF16)

    def gather_rows(own):
        parts = fetch_all(own, "x")
        return jnp.concatenate(parts + [swap(part, "c") for part in parts], 0)

    def scatter_rows(terms):
        own = terms[:512] + swap(terms[512:].astype(BF16), "c").astype(F32)
        total = own[:128]
        for j in (2, 1, 3):
            block = own[128 * j : 128 * j + 128].astype(BF16)
            total = total + shift(block, "x", j).astype(F32)
        return total

    norm_rows = gather_rows(norm_low)
    pre_act = dot(norm_rows, in_slice) + bias_slice
    activated = jax.nn.gelu(pre_act, approximate=False).astype(BF16)
    second_sum = first_norm + scatter_rows(dot(activated, fin_slice)) + full_bf
    normed_two, factor_two = norm_parts(second_sum)
    layer_out = (normed_two * full_g2 + full_s2).astype(BF16)
    grad_out = cotangent.astype(F32)
    d_gain_two = jnp.sum(grad_out * normed_two, 0)
    d_shift_two = jnp.sum(grad_out, 0)
    d_second = norm_back(grad_out * full_g2, normed_two, factor_two)
    d_second_low = d_second.astype(BF16)
    d_b_fin = column_sum(d_second_low)
    d_second_rows = gather_rows(d_second_low)
    d_pre = (times_trans(d_second_rows, fin_slice) * gelu_slope(pre_act)).astype(BF16)
    d_w_fin = outer_sum(activated, d_second_rows).astype(BF16)
    d_w_in = outer_sum(norm_rows, d_pre).astype(BF16)
    d_b_in = column_sum(d_pre)
    d_first_norm = scatter_rows(times_trans(d_pre, in_slice)) + d_second
    d_gain_one = jnp.sum(d_first_norm * normed_one, 0)
    d_shift_one = jnp.sum(d_first_norm, 0)
    d_first = norm_back(d_first_norm * full_g1, normed_one, factor_one)
    d_first_low = d_first.astype(BF16)
    d_w_out = outer_sum(attended, d_first_low).astype(BF16)
    d_b_out = column_sum(d_first_low)
    d_attended = times_trans(d_first_low, weight_out).astype(BF16)
    d_blocks = lax.all_to_all(
        d_attended.reshape(128, 16, 64).transpose(1, 0, 2),
        SEQ_AXES,
        split_axis=0,
        concat_axis=0,
        tiled=True,
    )

    vec = jnp.stack([d_b_out, d_gain_one, d_shift_one, d_b_fin, d_gain_two, d_shift_two])
    vec = vec.astype(BF16).reshape(6, 4, 2, 128).transpose(2, 1, 0, 3)
    vec = jnp.pad(vec.reshape(2, 4, 1, 768), ((0, 0), (0, 0), (0, 15), (0, 256)))
    out_terms = jnp.concatenate(
        [d_w_out.reshape(4, 2, 128, 1024).transpose(1, 0, 2, 3), vec], 2
    )
    out_pair = (
        lax.dynamic_index_in_dim(out_terms, c, 0, False).astype(F32)
        + swap(lax.dynamic_index_in_dim(out_terms, 1 - c, 0, False), "c").astype(F32)
    ).astype(BF16)
    out_sum = scatter_sum(
        lambda k: lax.dynamic_index_in_dim(out_pair, k, 0, False), "x", x
    ).astype(BF16)
    wout_part = out_sum[:128].reshape(16, 8, 2, 512).transpose(0, 2, 1, 3).reshape(16, 16, 512)
    vec_part = jnp.concatenate(
        [out_sum[128, :768].reshape(16, 48), d_b_in.astype(BF16).reshape(16, 32)], 1
    )
    vec_part = jnp.pad(vec_part.reshape(16, 1, 80), ((0, 0), (0, 15), (0, 432)))
    plane = jnp.concatenate(
        [
            d_w_in.reshape(4, 16, 16, 512).transpose(1, 0, 2, 3).reshape(16, 64, 512),
            d_w_fin.reshape(16, 32, 2, 512).transpose(0, 2, 1, 3).reshape(16, 64, 512),
            wout_part,
            vec_part,
        ],
        1,
    ).reshape(4, 4, 160, 512)
    plane = scatter_sum(
        lambda k: lax.dynamic_index_in_dim(plane, k, 0, False), Y_AXES, y
    ).astype(BF16)
    plane = scatter_sum(
        lambda k: lax.dynamic_index_in_dim(plane, k, 0, False), Z_AXES, z
    ).astype(BF16)
    in_part = plane[:64].reshape(4, 16, 512)
    in_part = [
        shift(lax.dynamic_index_in_dim(in_part, (x + j) % 4, 0, False), "x", j) if j else
        lax.dynamic_index_in_dim(in_part, x, 0, False)
        for j in range(4)
    ]
    plane = jnp.concatenate(in_part + [plane[64:]], 0)

    def gather_plane(own):
        column = jnp.stack(fetch_all(own, Z_AXES))
        parts = fetch_all(column, Y_AXES)
        return parts + [swap(part, "c") for part in parts]

    g_w_in, g_w_fin, g_w_out, g_vec = lay(
        lay_ffn_kernel,
        where,
        gather_plane(plane),
        [(256, 4096), (1024, 1024), (256, 1024), (32, 8, 128)],
        "lay_ffn",
    )
    g_vec = g_vec[:, 0, :80]
    g_six = g_vec[:, :48].reshape(2, 6, 128).transpose(1, 0, 2).reshape(6, 256)
    g_b_in = g_vec[:, 48:].reshape(1024)

    d_rel, d_abs = attend_back(place, q_wide, k_wide, v_wide, attf, d_blocks)
    d_back = lax.all_to_all(d_abs, SEQ_AXES, split_axis=0, concat_axis=0, tiled=True)
    d_projected = (
        d_back.reshape(16, 128, 3, 64).transpose(1, 2, 0, 3).reshape(128, 3072)
    )
    grad_tokens = times_trans(d_projected, weight_qkv) + d_first

    d_head = outer_sum(jnp.concatenate(pieces, 0), d_rel)
    bias_row = jnp.pad(column_sum(d_rel).reshape(1, 1, 1, 192), ((0, 0), (0, 0), (0, 7), (0, 0)))
    d_head = jnp.concatenate(
        [d_head.reshape(4, 2, 128, 192), jnp.broadcast_to(bias_row, (4, 2, 8, 192))], 2
    ).astype(BF16)
    d_head = scatter_sum(
        lambda k: lax.dynamic_index_in_dim(d_head, k, 0, False), "x", x
    )
    d_head = lax.dynamic_index_in_dim(d_head, zh, 0, False) + swap(
        lax.dynamic_index_in_dim(d_head, 1 - zh, 0, False).astype(BF16), "zh"
    ).astype(F32)
    g_w_qkv, g_b_qkv = lay(
        lay_qkv_kernel,
        where,
        gather_plane(d_head.astype(BF16)),
        [(256, 3072), (8, 3072)],
        "lay_qkv",
    )
    g_b_q = lax.dynamic_slice(g_b_qkv[0], (x * 256,), (256,))
    g_b_v = lax.dynamic_slice(g_b_qkv[0], (2048 + x * 256,), (256,))
    return (
        layer_out,
        grad_tokens,
        g_w_qkv,
        g_b_q,
        g_b_v,
        g_w_out,
        g_six[0],
        g_six[1],
        g_six[2],
        g_w_in,
        g_b_in,
        g_w_fin,
        g_six[3],
        g_six[4],
        g_six[5],
    )


def solution(mesh):
    fine = Mesh(mesh.devices.reshape(SIZES), AXES)
    rows = P(AXES, None)
    matrix = P("x", None)
    vector = P("x")
    in_specs = (
        rows,
        matrix,
        vector,
        vector,
        matrix,
        vector,
        vector,
        vector,
        matrix,
        vector,
        matrix,
        vector,
        vector,
        vector,
        rows,
    )
    out_specs = (
        rows,
        rows,
        matrix,
        vector,
        vector,
        matrix,
        vector,
        vector,
        vector,
        matrix,
        vector,
        matrix,
        vector,
        vector,
        vector,
    )
    return jax.shard_map(shards, mesh=fine, in_specs=in_specs, out_specs=out_specs, check_vma=False)
```

```python
import functools
import math

import jax
import jax.numpy as jnp
from jax import lax
from jax.experimental import pallas as pl
from jax.experimental.pallas import tpu as pltpu
from jax.sharding import Mesh, PartitionSpec as P

AXES = ("x", "zh", "zl", "yl", "c", "yh")
SIZES = (4, 2, 2, 2, 2, 2)
SEQ_AXES = ("zl", "yl", "c", "yh")
Y_AXES = ("yl", "yh")
Z_AXES = ("zh", "zl")
PLANE_AXES = ("zh", "zl", "yl", "yh")
D = 1024
FF = 4096
HEAD_DIM = 64
F32 = jnp.float32
BF16 = jnp.bfloat16

norm_eps = 1e-12
inv_root_two = 1.0 / math.sqrt(2.0)
inv_root_tau = 1.0 / math.sqrt(2.0 * math.pi)


def y_slot(y):
    return (y % 2) * 2 + y // 2


def shift(value, axis, step):
    slot = y_slot if axis == Y_AXES else (lambda i: i)
    return lax.ppermute(value, axis, [(slot(i), slot((i + step) % 4)) for i in range(4)])


def swap(value, axis):
    return lax.ppermute(value, axis, [(0, 1), (1, 0)])


def fetch_all(value, axis):
    return [value] + [shift(value, axis, -j) for j in (1, 2, 3)]


def after(value, *others):
    return lax.optimization_barrier((value,) + others)[0]


def roll_blocks(blocks, me):
    twice = jnp.stack(blocks + blocks)
    return lax.dynamic_slice_in_dim(twice, (4 - me) % 4, 4, 0)


def dot(left_op, right_op):
    return jnp.dot(left_op, right_op, preferred_element_type=F32)


def outer_sum(left_op, right_op):
    return lax.dot_general(left_op, right_op, (((0,), (0,)), ((), ())), preferred_element_type=F32)


def times_trans(left_op, right_op):
    return lax.dot_general(left_op, right_op, (((1,), (1,)), ((), ())), preferred_element_type=F32)


def norm_parts(summed):
    row_mean = jnp.mean(summed, -1, keepdims=True)
    centered = summed - row_mean
    factor = lax.rsqrt(jnp.mean(centered * centered, -1, keepdims=True) + norm_eps)
    return (centered * factor, factor)


def norm_back(scaled_grad, normed, factor):
    return factor * (
        scaled_grad
        - jnp.mean(scaled_grad, -1, keepdims=True)
        - normed * jnp.mean(scaled_grad * normed, -1, keepdims=True)
    )


def gelu_slope(pre_act):
    return (
        0.5 * (1.0 + lax.erf(pre_act * inv_root_two))
        + pre_act * jnp.exp(-0.5 * pre_act * pre_act) * inv_root_tau
    )


def column_sum(values):
    return jnp.sum(values.astype(F32), 0)


def three_terms(column):
    high = column.astype(BF16).astype(F32)
    rest = column - high
    middle = rest.astype(BF16).astype(F32)
    return high, middle, rest - middle


def widen(values, column):
    rows = values.shape[0]
    lane = lax.broadcasted_iota(jnp.int32, (rows, HEAD_DIM), 1)
    high, middle, low = three_terms(-column)
    extra = jnp.where(lane == 0, high, jnp.where(lane == 1, middle, jnp.where(lane == 2, low, 0.0)))
    return jnp.concatenate([values.astype(F32), extra], 1).astype(BF16)


def with_ones(values):
    rows = values.shape[0]
    lane = lax.broadcasted_iota(jnp.int32, (rows, HEAD_DIM), 1)
    return jnp.concatenate([values.astype(F32), jnp.where(lane < 3, 1.0, 0.0)], 1).astype(BF16)


PIECE_ROWS = (256,) * 8


def attend_kernel(place, *refs):
    pieces = refs[:8]
    blocks = refs[8:12]
    bias, q_out, k_out, v_out, attf_out, att_out, weight = refs[12:]
    for j in range(4):
        weight[(place[16] + j) % 4] = blocks[j][...]
    whole = weight[...].reshape(1024, 256)
    start = 0
    for piece, count in zip(pieces, PIECE_ROWS):
        proj = dot(piece[...], whole) + bias[...]
        rows = pl.ds(start, count)
        query = proj[:, :64].astype(BF16).astype(F32) * 0.125
        q_out[rows, :] = jnp.concatenate([query, jnp.zeros_like(query)], 1).astype(BF16)
        k_out[rows, :] = with_ones(proj[:, 64:128])
        v_out[rows, :] = with_ones(proj[:, 128:192])
        start += count

    @pl.loop(0, 8)
    def _(i):
        rows = pl.ds(pl.multiple_of(256 * i, 256), 256)
        query = q_out[rows, :]
        scores = times_trans(query, k_out[...])
        top = jnp.max(scores, 1, keepdims=True)
        probs = jnp.exp(scores - top).astype(BF16)
        weighted = dot(probs, v_out[...])
        total = weighted[:, 64:65]
        attended = weighted[:, :64] / total
        q_out[rows, :] = widen(query[:, :64], top + jnp.log(total))
        attf_out[rows, :] = attended
        low = attended.astype(BF16)
        att_out[place[2 * i]] = low[:128]
        att_out[place[2 * i + 1]] = low[128:]


def attend(place, pieces, blocks, bias):
    vmem = pl.BlockSpec(memory_space=pltpu.VMEM)
    wide = jax.ShapeDtypeStruct((2048, 128), BF16)
    return pl.pallas_call(
        attend_kernel,
        in_specs=[pl.BlockSpec(memory_space=pltpu.SMEM)] + [vmem] * 13,
        out_specs=[vmem] * 5,
        out_shape=[
            wide,
            wide,
            wide,
            jax.ShapeDtypeStruct((2048, 64), F32),
            jax.ShapeDtypeStruct((16, 128, 64), BF16),
        ],
        scratch_shapes=[pltpu.VMEM((4, 256, 256), BF16)],
        compiler_params=pltpu.CompilerParams(vmem_limit_bytes=24 * 2**20),
        cost_estimate=pl.CostEstimate(flops=3 * 10**9, bytes_accessed=6 * 10**6, transcendentals=2**22),
        name="attend",
    )(place, *pieces, *blocks, bias)


def attend_back_kernel(place, q_ref, k_ref, v_ref, attf, dout, *refs):
    pieces = refs[:8]
    abs_out, head_out, g_wide, dq_acc, rel = refs[8:]
    for r in range(16):
        rows = pl.ds(128 * r, 128)
        grad = dout[place[r]]
        delta = jnp.sum(grad.astype(F32) * attf[rows, :], 1, keepdims=True)
        g_wide[rows, :] = widen(grad, delta)
    dq_acc[...] = jnp.zeros_like(dq_acc)

    @pl.loop(0, 8)
    def _(j):
        rows = pl.ds(pl.multiple_of(256 * j, 256), 256)
        keys = k_ref[rows, :]
        probs = jnp.exp(times_trans(keys, q_ref[...]))
        d_less = times_trans(v_ref[rows, :], g_wide[...])
        d_scores = (probs * d_less).astype(BF16)
        d_val = dot(probs.astype(BF16), g_wide[...])[:, :64]
        d_key = dot(d_scores, q_ref[...])[:, :64]
        dq_acc[...] += outer_sum(keys, d_scores)
        rel[rows, :] = jnp.concatenate([jnp.zeros_like(d_key), d_key, d_val], 1).astype(BF16)

    sums = jnp.zeros((1, 192), F32)
    d_queries = (dq_acc[:64, :] * 0.125).T
    for r in range(16):
        rows = pl.ds(128 * r, 128)
        d_query = d_queries[128 * r : 128 * r + 128].astype(BF16)
        both = jnp.concatenate([d_query, rel[rows, :][:, 64:192]], 1)
        rel[rows, :] = both
        abs_out[place[r]] = both
        sums = sums + jnp.sum(both.astype(F32), 0, keepdims=True)

    grad = jnp.zeros((192, 1024), F32)
    start = 0
    for piece, count in zip(pieces, PIECE_ROWS):
        grad = grad + outer_sum(rel[start : start + count, :], piece[...])
        start += count
    grad = grad.T
    row = lax.broadcasted_iota(jnp.int32, (16, 128), 0)
    tail = jnp.where(
        row == 0,
        sums[:, :128],
        jnp.where(
            row == 1, jnp.concatenate([sums[:, 128:], jnp.zeros((1, 64), F32)], 1), 0.0
        ),
    ).astype(BF16)
    for owner in range(8):
        rows = grad[128 * owner : 128 * owner + 128]
        for part in range(3):
            cols = rows[:, 64 * part : 64 * part + 64]
            head_out[owner, 64 * part : 64 * part + 64, :] = jnp.concatenate(
                [cols[:64], cols[64:]], 1
            ).astype(BF16)
        head_out[owner, 192:208, :] = tail


def attend_back(place, q_wide, k_wide, v_wide, attf, dout, pieces):
    vmem = pl.BlockSpec(memory_space=pltpu.VMEM)
    return pl.pallas_call(
        attend_back_kernel,
        in_specs=[pl.BlockSpec(memory_space=pltpu.SMEM)] + [vmem] * 13,
        out_specs=[vmem] * 2,
        out_shape=[
            jax.ShapeDtypeStruct((16, 128, 192), BF16),
            jax.ShapeDtypeStruct((8, 208, 128), BF16),
        ],
        scratch_shapes=[
            pltpu.VMEM((2048, 128), BF16),
            pltpu.VMEM((128, 2048), F32),
            pltpu.VMEM((2048, 192), BF16),
        ],
        compiler_params=pltpu.CompilerParams(vmem_limit_bytes=24 * 2**20),
        cost_estimate=pl.CostEstimate(flops=10**10, bytes_accessed=8 * 10**6, transcendentals=2**22),
        name="attend_back",
    )(place, q_wide, k_wide, v_wide, attf, dout, *pieces)


def chip_row(y, z):
    return z * 4 + y_slot(y)


def lay_ffn_kernel(where, *refs):
    grads = refs[:8]
    win_out, wfin_out = refs[8:]
    x, y, z, c = where[0], where[1], where[2], where[3]
    for cj in range(2):
        core = (c + cj) % 2
        for yj in range(4):
            for zj in range(4):
                chip = chip_row((y + yj) % 4, (z + zj) % 4)
                piece = grads[cj * 4 + zj]
                for xj in range(4):
                    owner = (x + 4 - xj) % 4
                    col = pl.multiple_of(owner * 1024 + core * 512, 512)
                    win_out[pl.ds(pl.multiple_of(chip * 16, 16), 16), pl.ds(col, 512)] = piece[
                        yj, 16 * xj : 16 * xj + 16
                    ].astype(F32)
                for half in range(2):
                    wfin_out[
                        pl.ds(pl.multiple_of(core * 512 + chip * 32, 32), 32),
                        512 * half : 512 * half + 512,
                    ] = piece[yj, 64 + 32 * half : 96 + 32 * half].astype(F32)


def lay_rest_kernel(where, *refs):
    grads = refs[:8]
    w_out, b_out, wout_out, vec_out = refs[8:]
    y, z, c = where[1], where[2], where[3]
    for cj in range(2):
        core = (c + cj) % 2
        for yj in range(2):
            y_now = (y + yj) % 4
            swapped = y_now // 2 == 1
            for zj in range(4):
                z_now = (z + zj) % 4
                first = grads[cj * 4 + yj][zj, :208, :].astype(F32)
                second = grads[cj * 4 + yj + 2][zj, :208, :].astype(F32)
                low = jnp.where(swapped, second, first)
                high = jnp.where(swapped, first, second)
                head = (z_now % 2) * 8 + (y_now % 2) * 4 + core * 2
                for part in range(3):
                    rows = slice(part * 64, part * 64 + 64)
                    col = pl.multiple_of(part * 1024 + head * 64, 128)
                    base = (z_now // 2) * 128
                    for half in range(2):
                        lanes = slice(half * 64, half * 64 + 64)
                        w_out[
                            pl.ds(pl.multiple_of(base + half * 64, 64), 64), pl.ds(col, 128)
                        ] = jnp.concatenate([low[rows, lanes], high[rows, lanes]], 1)
                    if part != 1:
                        row = 192 + part // 2
                        b_out[:, pl.ds(col, 128)] = jnp.concatenate(
                            [low[row : row + 1, :64], high[row : row + 1, :64]], 1
                        )
        for yj in range(4):
            for zj in range(4):
                chip = chip_row((y + yj) % 4, (z + zj) % 4)
                rest = grads[cj * 4 + yj][zj, 208:288, :].astype(F32)
                for lanes in range(8):
                    wout_out[
                        pl.ds(pl.multiple_of(core * 128 + chip * 8, 8), 8),
                        128 * lanes : 128 * lanes + 128,
                    ] = rest[8 * lanes : 8 * lanes + 8]
                vec_out[core * 16 + chip] = rest[64:72]


def lay(kernel, where, grads, shapes, name):
    vmem = pl.BlockSpec(memory_space=pltpu.VMEM)
    return pl.pallas_call(
        kernel,
        in_specs=[pl.BlockSpec(memory_space=pltpu.SMEM)] + [vmem] * len(grads),
        out_specs=[vmem] * len(shapes),
        out_shape=[jax.ShapeDtypeStruct(s, F32) for s in shapes],
        compiler_params=pltpu.CompilerParams(vmem_limit_bytes=24 * 2**20),
        cost_estimate=pl.CostEstimate(flops=10**6, bytes_accessed=15 * 10**6, transcendentals=0),
        name=name,
    )(where, *grads)


def plane_sum(terms):
    sent = lax.all_to_all(terms, PLANE_AXES, split_axis=0, concat_axis=0, tiled=True)
    return jnp.sum(sent.astype(F32), 0).astype(BF16)


def order_kernel(where, *refs):
    for j in range(4):
        refs[4][(where[0] + j) % 4] = refs[j][...]


def order_blocks(where, blocks):
    vmem = pl.BlockSpec(memory_space=pltpu.VMEM)
    rows, width = blocks[0].shape
    whole = pl.pallas_call(
        order_kernel,
        in_specs=[pl.BlockSpec(memory_space=pltpu.SMEM)] + [vmem] * 4,
        out_specs=vmem,
        out_shape=jax.ShapeDtypeStruct((4, rows, width), BF16),
        compiler_params=pltpu.CompilerParams(vmem_limit_bytes=24 * 2**20),
        name="order_blocks",
    )(where, *blocks)
    return whole.reshape(4 * rows, width)


def shards(
    tokens,
    w_qkv,
    bias_q,
    bias_v,
    w_out,
    bias_o,
    gain_attn,
    shift_attn,
    w_in,
    bias_in,
    w_fin,
    bias_fin,
    gain_ffn,
    shift_ffn,
    cotangent,
):
    x = lax.axis_index("x")
    zh = lax.axis_index("zh")
    zl = lax.axis_index("zl")
    yl = lax.axis_index("yl")
    c = lax.axis_index("c")
    yh = lax.axis_index("yh")
    y = yh * 2 + yl
    z = zh * 2 + zl
    head = zl * 8 + yl * 4 + c * 2 + yh
    where = jnp.stack([x, y, z, c]).astype(jnp.int32)
    places = []
    for cj in range(2):
        for yj in range(4):
            for zj in range(2):
                y_now = (y + yj) % 4
                places.append(((zl + zj) % 2) * 8 + (y_now % 2) * 4 + ((c + cj) % 2) * 2 + y_now // 2)
    place = jnp.stack(places + [x]).astype(jnp.int32)

    pair = jnp.concatenate([tokens, swap(tokens, "zl")], 0)
    mine = fetch_all(pair, Y_AXES)
    pieces = mine + [swap(part, "c") for part in mine]
    w_late = after(w_qkv, pair)
    vectors = jnp.stack(
        [bias_q, bias_v, bias_o, gain_attn, shift_attn, bias_fin, gain_ffn, shift_ffn], 1
    )
    head_cols = jnp.concatenate(
        [lax.dynamic_slice(w_late, (0, part * 1024 + head * 64), (256, 64)) for part in range(3)]
        + [vectors, jnp.zeros((256, 56), BF16)],
        1,
    )
    head_blocks = fetch_all(head_cols, "x")
    full = roll_blocks([block[:, 192:200] for block in head_blocks], x)
    full = full.reshape(1024, 8).T.astype(F32)
    full_bq, full_bv, full_bo, full_g1, full_s1, full_bf, full_g2, full_s2 = [
        full[i] for i in range(8)
    ]

    def gather_columns(weight):
        width = weight.shape[1] // 2
        own = lax.dynamic_slice(weight, (0, c * width), (256, width))
        own = lax.all_gather(own, "x", axis=0, tiled=True)
        return own, swap(own, "c")

    def halves(values):
        width = values.shape[1] // 2
        return (
            lax.dynamic_slice(values, (0, c * width), (values.shape[0], width)),
            lax.dynamic_slice(values, (0, (1 - c) * width), (values.shape[0], width)),
        )

    out_own, out_other = gather_columns(w_out)
    w_in = after(w_in, pieces[1])
    qkv_own, qkv_other = gather_columns(w_qkv)

    in_blocks = []
    for j in range(4):
        part = lax.dynamic_slice(w_in, (0, ((x + j) % 4) * 1024 + c * 512), (256, 512))
        in_blocks.append(part if j == 0 else shift(part, "x", j))
    fin_slice = lax.dynamic_slice(w_fin, (c * 512, 0), (512, 1024))
    bias_slice = lax.dynamic_slice(bias_in, (c * 512,), (512,)).astype(F32)

    bias_head = jnp.concatenate(
        [
            lax.dynamic_slice(full_bq, (head * 64,), (64,)),
            jnp.zeros((64,), F32),
            lax.dynamic_slice(full_bv, (head * 64,), (64,)),
            jnp.zeros((64,), F32),
        ]
    ).reshape(1, 256)
    q_wide, k_wide, v_wide, attf, att_blocks = attend(place, pieces, head_blocks, bias_head)
    *in_blocks, _ = lax.optimization_barrier(tuple(in_blocks) + (att_blocks,))
    in_blocks = [in_blocks[0], in_blocks[3], in_blocks[2], in_blocks[1]]
    in_slice = order_blocks(where, in_blocks)
    attended = (
        lax.all_to_all(att_blocks, SEQ_AXES, split_axis=0, concat_axis=0, tiled=True)
        .transpose(1, 0, 2)
        .reshape(128, 1024)
    )

    attended = after(attended, qkv_own)
    branch_own, branch_other = dot(attended, out_own), dot(attended, out_other)
    branch = jnp.where(
        c == 0,
        jnp.concatenate([branch_own, branch_other], 1),
        jnp.concatenate([branch_other, branch_own], 1),
    )
    first_sum = tokens.astype(F32) + branch + full_bo
    normed_one, factor_one = norm_parts(first_sum)
    first_norm = normed_one * full_g1 + full_s1
    norm_low = first_norm.astype(BF16)

    def gather_rows(own):
        parts = fetch_all(own, "x")
        return jnp.concatenate(parts + [swap(part, "c") for part in parts], 0)

    def scatter_rows(terms):
        own = terms[:512] + swap(terms[512:].astype(BF16), "c").astype(F32)
        own = lax.optimization_barrier(own)
        total = own[:128]
        for j in (2, 1, 3):
            block = own[128 * j : 128 * j + 128].astype(BF16)
            total = total + shift(block, "x", j).astype(F32)
        return total, own

    norm_rows = gather_rows(norm_low)
    pre_act = dot(norm_rows, in_slice) + bias_slice
    activated = jax.nn.gelu(pre_act, approximate=False).astype(BF16)
    ffn_out, _ = scatter_rows(dot(activated, fin_slice))
    second_sum = first_norm + ffn_out + full_bf
    normed_two, factor_two = norm_parts(second_sum)
    layer_out = (normed_two * full_g2 + full_s2).astype(BF16)
    grad_out = cotangent.astype(F32)
    d_gain_two = jnp.sum(grad_out * normed_two, 0)
    d_shift_two = jnp.sum(grad_out, 0)
    d_second = norm_back(grad_out * full_g2, normed_two, factor_two)
    d_second_low = d_second.astype(BF16)
    d_b_fin = column_sum(d_second_low)
    d_second_low = after(d_second_low, qkv_other)
    d_second_rows = gather_rows(d_second_low)
    d_pre = (times_trans(d_second_rows, fin_slice) * gelu_slope(pre_act)).astype(BF16)
    d_norm, pair_sum = scatter_rows(times_trans(d_pre, in_slice))
    activated, norm_rows, d_pre = lax.optimization_barrier(
        (activated, norm_rows, d_pre, pair_sum)
    )[:3]
    d_w_fin = outer_sum(activated, d_second_rows).astype(BF16)
    d_w_in = outer_sum(norm_rows, d_pre).astype(BF16)
    fin_terms = d_w_fin.reshape(16, 32, 1024)
    in_terms = d_w_in.reshape(4, 16, 16, 512).transpose(1, 0, 2, 3).reshape(16, 64, 512)
    fin_sum = plane_sum(fin_terms)
    d_norm = after(d_norm, fin_terms, in_terms)
    d_b_in = column_sum(d_pre)
    d_first_norm = d_norm + d_second
    d_gain_one = jnp.sum(d_first_norm * normed_one, 0)
    d_shift_one = jnp.sum(d_first_norm, 0)
    d_first = norm_back(d_first_norm * full_g1, normed_one, factor_one)
    d_first_low = d_first.astype(BF16)
    d_first_low = after(d_first_low, fin_sum)
    low_own, low_other = halves(d_first_low)
    d_attended = (times_trans(low_own, out_own) + times_trans(low_other, out_other)).astype(BF16)
    attended, d_first_low = lax.optimization_barrier((attended, d_first_low, d_attended))[:2]
    d_w_out = outer_sum(attended, d_first_low).astype(BF16)
    d_b_out = column_sum(d_first_low)
    d_blocks = lax.all_to_all(
        d_attended.reshape(128, 16, 64).transpose(1, 0, 2),
        SEQ_AXES,
        split_axis=0,
        concat_axis=0,
        tiled=True,
    )

    vec = jnp.stack([d_b_out, d_gain_one, d_shift_one, d_b_fin, d_gain_two, d_shift_two])
    vec = vec.astype(BF16).reshape(6, 4, 2, 128).transpose(2, 1, 0, 3)
    vec = jnp.pad(vec.reshape(2, 4, 1, 768), ((0, 0), (0, 0), (0, 15), (0, 256)))
    out_terms = jnp.concatenate(
        [d_w_out.reshape(4, 2, 128, 1024).transpose(1, 0, 2, 3), vec], 2
    )
    out_pair = (
        lax.dynamic_index_in_dim(out_terms, c, 0, False).astype(F32)
        + swap(lax.dynamic_index_in_dim(out_terms, 1 - c, 0, False), "c").astype(F32)
    ).astype(BF16)
    in_sum = plane_sum(after(in_terms, d_blocks))
    out_late = after(out_pair, d_blocks)
    out_sum = lax.dynamic_index_in_dim(out_pair, x, 0, False).astype(F32)
    for j in (2, 1, 3):
        block = lax.dynamic_index_in_dim(out_late, (x + j) % 4, 0, False)
        out_sum = out_sum + shift(block, "x", j).astype(F32)
    d_abs, d_head = attend_back(place, q_wide, k_wide, v_wide, attf, d_blocks, pieces)
    d_head = lax.all_to_all(d_head, ("x", "zh"), split_axis=0, concat_axis=0, tiled=True)

    out_sum = after(out_sum, d_abs)
    out_sum = out_sum.astype(BF16)
    vec_part = jnp.concatenate(
        [out_sum[128, :768].reshape(16, 48), d_b_in.astype(BF16).reshape(16, 32)], 1
    )
    vec_part = jnp.pad(vec_part.reshape(16, 1, 80), ((0, 0), (0, 15), (0, 48)))
    rest = jnp.concatenate(
        [out_sum[:128].reshape(16, 8, 8, 128).transpose(0, 2, 1, 3).reshape(16, 64, 128), vec_part],
        1,
    )
    rest = plane_sum(rest)

    in_sum = after(in_sum, d_abs)
    in_part = in_sum.reshape(4, 16, 512)
    in_part = [
        shift(lax.dynamic_index_in_dim(in_part, (x + j) % 4, 0, False), "x", j) if j else
        lax.dynamic_index_in_dim(in_part, x, 0, False)
        for j in range(4)
    ]
    plane = jnp.concatenate(in_part + [fin_sum[:, :512], fin_sum[:, 512:]], 0)
    plane_row = jnp.stack(fetch_all(plane, Y_AXES))
    plane_parts = fetch_all(plane_row, Z_AXES)

    rest = jnp.concatenate([jnp.sum(d_head.astype(F32), 0).astype(BF16), rest], 0)
    rest_column = jnp.stack(fetch_all(rest, Z_AXES))
    rest_parts = fetch_all(rest_column, Y_AXES)

    d_abs = after(d_abs, rest)
    d_back = lax.all_to_all(d_abs, SEQ_AXES, split_axis=0, concat_axis=0, tiled=True)
    d_projected = d_back.reshape(16, 128, 3, 64).transpose(1, 2, 0, 3).reshape(128, 3072)
    proj_own, proj_other = halves(d_projected)
    grad_tokens = times_trans(proj_own, qkv_own) + times_trans(proj_other, qkv_other) + d_first

    g_w_in, g_w_fin = lay(
        lay_ffn_kernel,
        where,
        plane_parts + [swap(part, "c") for part in plane_parts],
        [(256, 4096), (1024, 1024)],
        "lay_ffn",
    )
    g_w_qkv, g_b_qkv, g_w_out, g_vec = lay(
        lay_rest_kernel,
        where,
        list(
            lax.optimization_barrier(
                tuple(rest_parts + [swap(part, "c") for part in rest_parts]) + (g_w_in,)
            )
        )[:8],
        [(256, 3072), (1, 3072), (256, 1024), (32, 8, 128)],
        "lay_rest",
    )
    g_vec = g_vec[:, 0, :80]
    g_six = g_vec[:, :48].reshape(2, 6, 128).transpose(1, 0, 2).reshape(6, 256)
    g_b_in = g_vec[:, 48:].reshape(1024)
    g_b_q = lax.dynamic_slice(g_b_qkv[0], (x * 256,), (256,))
    g_b_v = lax.dynamic_slice(g_b_qkv[0], (2048 + x * 256,), (256,))
    return (
        layer_out,
        grad_tokens,
        g_w_qkv,
        g_b_q,
        g_b_v,
        g_w_out,
        g_six[0],
        g_six[1],
        g_six[2],
        g_w_in,
        g_b_in,
        g_w_fin,
        g_six[3],
        g_six[4],
        g_six[5],
    )


def solution(mesh):
    fine = Mesh(mesh.devices.reshape(SIZES), AXES)
    rows = P(AXES, None)
    matrix = P("x", None)
    vector = P("x")
    in_specs = (
        rows,
        matrix,
        vector,
        vector,
        matrix,
        vector,
        vector,
        vector,
        matrix,
        vector,
        matrix,
        vector,
        vector,
        vector,
        rows,
    )
    out_specs = (
        rows,
        rows,
        matrix,
        vector,
        vector,
        matrix,
        vector,
        vector,
        vector,
        matrix,
        vector,
        matrix,
        vector,
        vector,
        vector,
    )
    return jax.shard_map(shards, mesh=fine, in_specs=in_specs, out_specs=out_specs, check_vma=False)
```

```python
import functools
import math

import jax
import jax.numpy as jnp
from jax import lax
from jax.experimental import pallas as pl
from jax.experimental.pallas import tpu as pltpu
from jax.sharding import Mesh, PartitionSpec as P

AXES = ("x", "zh", "zl", "yl", "c", "yh")
SIZES = (4, 2, 2, 2, 2, 2)
SEQ_AXES = ("zl", "yl", "c", "yh")
Y_AXES = ("yl", "yh")
Z_AXES = ("zh", "zl")
PLANE_AXES = ("zh", "zl", "yl", "yh")
D = 1024
FF = 4096
HEAD_DIM = 64
F32 = jnp.float32
BF16 = jnp.bfloat16

norm_eps = 1e-12
inv_root_two = 1.0 / math.sqrt(2.0)
inv_root_tau = 1.0 / math.sqrt(2.0 * math.pi)


def y_slot(y):
    return (y % 2) * 2 + y // 2


def shift(value, axis, step):
    slot = y_slot if axis == Y_AXES else (lambda i: i)
    return lax.ppermute(value, axis, [(slot(i), slot((i + step) % 4)) for i in range(4)])


def swap(value, axis):
    return lax.ppermute(value, axis, [(0, 1), (1, 0)])


def fetch_all(value, axis):
    return [value] + [shift(value, axis, -j) for j in (1, 2, 3)]


def after(value, *others):
    return lax.optimization_barrier((value,) + others)[0]


def roll_blocks(blocks, me):
    twice = jnp.stack(blocks + blocks)
    return lax.dynamic_slice_in_dim(twice, (4 - me) % 4, 4, 0)


def dot(left_op, right_op):
    return jnp.dot(left_op, right_op, preferred_element_type=F32)


def outer_sum(left_op, right_op):
    return lax.dot_general(left_op, right_op, (((0,), (0,)), ((), ())), preferred_element_type=F32)


def times_trans(left_op, right_op):
    return lax.dot_general(left_op, right_op, (((1,), (1,)), ((), ())), preferred_element_type=F32)


def norm_parts(summed):
    row_mean = jnp.mean(summed, -1, keepdims=True)
    centered = summed - row_mean
    factor = lax.rsqrt(jnp.mean(centered * centered, -1, keepdims=True) + norm_eps)
    return (centered * factor, factor)


def norm_back(scaled_grad, normed, factor):
    return factor * (
        scaled_grad
        - jnp.mean(scaled_grad, -1, keepdims=True)
        - normed * jnp.mean(scaled_grad * normed, -1, keepdims=True)
    )


def gelu_slope(pre_act):
    return (
        0.5 * (1.0 + lax.erf(pre_act * inv_root_two))
        + pre_act * jnp.exp(-0.5 * pre_act * pre_act) * inv_root_tau
    )


def column_sum(values):
    return jnp.sum(values.astype(F32), 0)


def three_terms(column):
    high = column.astype(BF16).astype(F32)
    rest = column - high
    middle = rest.astype(BF16).astype(F32)
    return high, middle, rest - middle


def widen(values, column):
    rows = values.shape[0]
    lane = lax.broadcasted_iota(jnp.int32, (rows, HEAD_DIM), 1)
    high, middle, low = three_terms(-column)
    extra = jnp.where(lane == 0, high, jnp.where(lane == 1, middle, jnp.where(lane == 2, low, 0.0)))
    return jnp.concatenate([values.astype(F32), extra], 1).astype(BF16)


def with_ones(values):
    rows = values.shape[0]
    lane = lax.broadcasted_iota(jnp.int32, (rows, HEAD_DIM), 1)
    return jnp.concatenate([values.astype(F32), jnp.where(lane < 3, 1.0, 0.0)], 1).astype(BF16)


PIECE_ROWS = (256,) * 8


def attend_kernel(place, *refs):
    pieces = refs[:8]
    blocks = refs[8:12]
    bias, q_out, k_out, v_out, attf_out, att_out, weight = refs[12:]
    for j in range(4):
        weight[(place[16] + j) % 4] = blocks[j][...]
    whole = weight[...].reshape(1024, 256)
    start = 0
    for piece, count in zip(pieces, PIECE_ROWS):
        proj = dot(piece[...], whole) + bias[...]
        rows = pl.ds(start, count)
        query = proj[:, :64].astype(BF16).astype(F32) * 0.125
        q_out[rows, :] = jnp.concatenate([query, jnp.zeros_like(query)], 1).astype(BF16)
        k_out[rows, :] = with_ones(proj[:, 64:128])
        v_out[rows, :] = with_ones(proj[:, 128:192])
        start += count

    @pl.loop(0, 8, unroll=2)
    def _(i):
        rows = pl.ds(pl.multiple_of(256 * i, 256), 256)
        query = q_out[rows, :]
        scores = times_trans(query, k_out[...])
        top = jnp.max(scores, 1, keepdims=True)
        probs = jnp.exp(scores - top).astype(BF16)
        weighted = dot(probs, v_out[...])
        total = weighted[:, 64:65]
        attended = weighted[:, :64] / total
        q_out[rows, :] = widen(query[:, :64], top + jnp.log(total))
        attf_out[rows, :] = attended
        low = attended.astype(BF16)
        att_out[place[2 * i]] = low[:128]
        att_out[place[2 * i + 1]] = low[128:]


def attend(place, pieces, blocks, bias):
    vmem = pl.BlockSpec(memory_space=pltpu.VMEM)
    wide = jax.ShapeDtypeStruct((2048, 128), BF16)
    return pl.pallas_call(
        attend_kernel,
        in_specs=[pl.BlockSpec(memory_space=pltpu.SMEM)] + [vmem] * 13,
        out_specs=[vmem] * 5,
        out_shape=[
            wide,
            wide,
            wide,
            jax.ShapeDtypeStruct((2048, 64), F32),
            jax.ShapeDtypeStruct((16, 128, 64), BF16),
        ],
        scratch_shapes=[pltpu.VMEM((4, 256, 256), BF16)],
        compiler_params=pltpu.CompilerParams(vmem_limit_bytes=24 * 2**20),
        cost_estimate=pl.CostEstimate(flops=3 * 10**9, bytes_accessed=6 * 10**6, transcendentals=2**22),
        name="attend",
    )(place, *pieces, *blocks, bias)


def attend_back_kernel(place, q_ref, k_ref, v_ref, attf, dout, *refs):
    pieces = refs[:8]
    abs_out, head_out, g_wide, dq_acc, rel, held, arrived = refs[8:]
    copies = [pltpu.make_async_copy(pieces[i], held.at[i], arrived.at[i]) for i in range(8)]
    for copy in copies:
        copy.start()
    for r in range(16):
        rows = pl.ds(128 * r, 128)
        grad = dout[place[r]]
        delta = jnp.sum(grad.astype(F32) * attf[rows, :], 1, keepdims=True)
        g_wide[rows, :] = widen(grad, delta)
    dq_acc[...] = jnp.zeros_like(dq_acc)

    @pl.loop(0, 8, unroll=2)
    def _(j):
        rows = pl.ds(pl.multiple_of(256 * j, 256), 256)
        keys = k_ref[rows, :]
        probs = jnp.exp(times_trans(keys, q_ref[...]))
        d_less = times_trans(v_ref[rows, :], g_wide[...])
        d_scores = (probs * d_less).astype(BF16)
        d_val = dot(probs.astype(BF16), g_wide[...])[:, :64]
        d_key = dot(d_scores, q_ref[...])[:, :64]
        dq_acc[...] += outer_sum(keys, d_scores)
        rel[rows, :] = jnp.concatenate([jnp.zeros_like(d_key), d_key, d_val], 1).astype(BF16)

    sums = jnp.zeros((1, 192), F32)
    d_queries = (dq_acc[:64, :] * 0.125).T
    for r in range(16):
        rows = pl.ds(128 * r, 128)
        d_query = d_queries[128 * r : 128 * r + 128].astype(BF16)
        both = jnp.concatenate([d_query, rel[rows, :][:, 64:192]], 1)
        rel[rows, :] = both
        abs_out[place[r]] = both
        sums = sums + jnp.sum(both.astype(F32), 0, keepdims=True)

    grad = jnp.zeros((192, 1024), F32)
    for i in range(8):
        copies[i].wait()
        grad = grad + outer_sum(rel[256 * i : 256 * i + 256, :], held[i])
    grad = grad.T
    row = lax.broadcasted_iota(jnp.int32, (16, 128), 0)
    tail = jnp.where(
        row == 0,
        sums[:, :128],
        jnp.where(
            row == 1, jnp.concatenate([sums[:, 128:], jnp.zeros((1, 64), F32)], 1), 0.0
        ),
    ).astype(BF16)
    for owner in range(8):
        rows = grad[128 * owner : 128 * owner + 128]
        for part in range(3):
            cols = rows[:, 64 * part : 64 * part + 64]
            head_out[owner, 64 * part : 64 * part + 64, :] = jnp.concatenate(
                [cols[:64], cols[64:]], 1
            ).astype(BF16)
        head_out[owner, 192:208, :] = tail


def attend_back(place, q_wide, k_wide, v_wide, attf, dout, pieces):
    vmem = pl.BlockSpec(memory_space=pltpu.VMEM)
    return pl.pallas_call(
        attend_back_kernel,
        in_specs=[pl.BlockSpec(memory_space=pltpu.SMEM)]
        + [vmem] * 5
        + [pl.BlockSpec(memory_space=pl.ANY)] * 8,
        out_specs=[vmem] * 2,
        out_shape=[
            jax.ShapeDtypeStruct((16, 128, 192), BF16),
            jax.ShapeDtypeStruct((8, 208, 128), BF16),
        ],
        scratch_shapes=[
            pltpu.VMEM((2048, 128), BF16),
            pltpu.VMEM((128, 2048), F32),
            pltpu.VMEM((2048, 192), BF16),
            pltpu.VMEM((8, 256, 1024), BF16),
            pltpu.SemaphoreType.DMA((8,)),
        ],
        compiler_params=pltpu.CompilerParams(vmem_limit_bytes=40 * 2**20),
        cost_estimate=pl.CostEstimate(flops=10**10, bytes_accessed=8 * 10**6, transcendentals=2**22),
        name="attend_back",
    )(place, q_wide, k_wide, v_wide, attf, dout, *pieces)


def chip_row(y, z):
    return z * 4 + y_slot(y)


def lay_fin_kernel(where, *refs):
    grads, out = refs[:8], refs[8]
    y, z, c = where[1], where[2], where[3]
    for cj in range(2):
        core = (c + cj) % 2
        for yj in range(4):
            for zj in range(4):
                chip = chip_row((y + yj) % 4, (z + zj) % 4)
                for half in range(2):
                    out[
                        pl.ds(pl.multiple_of(core * 512 + chip * 32, 32), 32),
                        512 * half : 512 * half + 512,
                    ] = grads[cj * 4 + yj][zj, 32 * half : 32 * half + 32].astype(F32)


def lay_ffn_kernel(where, *refs):
    grads = refs[:8]
    win_out, wout_out, vec_out = refs[8:]
    x, y, z, c = where[0], where[1], where[2], where[3]
    for cj in range(2):
        core = (c + cj) % 2
        for yj in range(4):
            for zj in range(4):
                chip = chip_row((y + yj) % 4, (z + zj) % 4)
                piece = grads[cj * 4 + zj]
                for xj in range(4):
                    owner = (x + 4 - xj) % 4
                    col = pl.multiple_of(owner * 1024 + core * 512, 512)
                    win_out[pl.ds(pl.multiple_of(chip * 16, 16), 16), pl.ds(col, 512)] = piece[
                        yj, 16 * xj : 16 * xj + 16
                    ].astype(F32)
                rest = piece[yj, 64:96].astype(F32)
                for half in range(2):
                    wout_out[
                        pl.ds(pl.multiple_of(core * 128 + chip * 8, 8), 8),
                        512 * half : 512 * half + 512,
                    ] = rest[8 * half : 8 * half + 8]
                vec_out[core * 16 + chip] = rest[16:24, 0:128]


def lay_qkv_kernel(where, *refs):
    grads = refs[:2]
    w_out, b_out = refs[2:]
    c = where[3]
    for cj in range(2):
        core = (c + cj) % 2
        for zz in range(4):
            for yl in range(2):
                chip = zz * 4 + yl * 2
                low = grads[cj][chip].astype(F32)
                high = grads[cj][chip + 1].astype(F32)
                head = (zz % 2) * 8 + yl * 4 + core * 2
                base = (zz // 2) * 128
                for part in range(3):
                    rows = slice(part * 64, part * 64 + 64)
                    col = pl.multiple_of(part * 1024 + head * 64, 128)
                    for half in range(2):
                        lanes = slice(half * 64, half * 64 + 64)
                        w_out[
                            base + half * 64 : base + half * 64 + 64, pl.ds(col, 128)
                        ] = jnp.concatenate([low[rows, lanes], high[rows, lanes]], 1)
                    if part != 1:
                        row = 192 + part // 2
                        b_out[:, pl.ds(col, 128)] = jnp.concatenate(
                            [low[row : row + 1, :64], high[row : row + 1, :64]], 1
                        )


def lay(kernel, where, grads, shapes, name):
    count = len(grads)

    def body(where_ref, *refs):
        sources, outs = refs[:count], refs[count : count + len(shapes)]
        held, arrived = refs[count + len(shapes) : -1], refs[-1]
        copies = [pltpu.make_async_copy(sources[i], held[i], arrived.at[i]) for i in range(count)]
        for copy in copies:
            copy.start()
        for copy in copies:
            copy.wait()
        kernel(where_ref, *held, *outs)

    vmem = pl.BlockSpec(memory_space=pltpu.VMEM)
    return pl.pallas_call(
        body,
        in_specs=[pl.BlockSpec(memory_space=pltpu.SMEM)]
        + [pl.BlockSpec(memory_space=pl.ANY)] * count,
        out_specs=[vmem] * len(shapes),
        out_shape=[jax.ShapeDtypeStruct(s, F32) for s in shapes],
        scratch_shapes=[pltpu.VMEM(g.shape, BF16) for g in grads]
        + [pltpu.SemaphoreType.DMA((count,))],
        compiler_params=pltpu.CompilerParams(vmem_limit_bytes=24 * 2**20),
        cost_estimate=pl.CostEstimate(flops=10**6, bytes_accessed=15 * 10**6, transcendentals=0),
        name=name,
    )(where, *grads)


def plane_sum(terms):
    sent = lax.all_to_all(terms, PLANE_AXES, split_axis=0, concat_axis=0, tiled=True)
    return jnp.sum(sent.astype(F32), 0).astype(BF16)


def order_kernel(where, *refs):
    for j in range(4):
        refs[4][(where[0] + j) % 4] = refs[j][...]


def order_blocks(where, blocks):
    vmem = pl.BlockSpec(memory_space=pltpu.VMEM)
    rows, width = blocks[0].shape
    whole = pl.pallas_call(
        order_kernel,
        in_specs=[pl.BlockSpec(memory_space=pltpu.SMEM)] + [vmem] * 4,
        out_specs=vmem,
        out_shape=jax.ShapeDtypeStruct((4, rows, width), BF16),
        compiler_params=pltpu.CompilerParams(vmem_limit_bytes=24 * 2**20),
        name="order_blocks",
    )(where, *blocks)
    return whole.reshape(4 * rows, width)


def shards(
    tokens,
    w_qkv,
    bias_q,
    bias_v,
    w_out,
    bias_o,
    gain_attn,
    shift_attn,
    w_in,
    bias_in,
    w_fin,
    bias_fin,
    gain_ffn,
    shift_ffn,
    cotangent,
):
    x = lax.axis_index("x")
    zh = lax.axis_index("zh")
    zl = lax.axis_index("zl")
    yl = lax.axis_index("yl")
    c = lax.axis_index("c")
    yh = lax.axis_index("yh")
    y = yh * 2 + yl
    z = zh * 2 + zl
    head = zl * 8 + yl * 4 + c * 2 + yh
    where = jnp.stack([x, y, z, c]).astype(jnp.int32)
    places = []
    for cj in range(2):
        for yj in range(4):
            for zj in range(2):
                y_now = (y + yj) % 4
                places.append(((zl + zj) % 2) * 8 + (y_now % 2) * 4 + ((c + cj) % 2) * 2 + y_now // 2)
    place = jnp.stack(places + [x]).astype(jnp.int32)

    pair = jnp.concatenate([tokens, swap(tokens, "zl")], 0)
    mine = fetch_all(pair, Y_AXES)
    pieces = mine + [swap(part, "c") for part in mine]
    w_late = after(w_qkv, pair)
    vectors = jnp.stack(
        [bias_q, bias_v, bias_o, gain_attn, shift_attn, bias_fin, gain_ffn, shift_ffn], 1
    )
    head_cols = jnp.concatenate(
        [lax.dynamic_slice(w_late, (0, part * 1024 + head * 64), (256, 64)) for part in range(3)]
        + [vectors, jnp.zeros((256, 56), BF16)],
        1,
    )
    head_blocks = fetch_all(head_cols, "x")
    full = roll_blocks([block[:, 192:200] for block in head_blocks], x)
    full = full.reshape(1024, 8).T.astype(F32)
    full_bq, full_bv, full_bo, full_g1, full_s1, full_bf, full_g2, full_s2 = [
        full[i] for i in range(8)
    ]

    def gather_columns(weight):
        width = weight.shape[1] // 2
        own = lax.dynamic_slice(weight, (0, c * width), (256, width))
        own = lax.all_gather(own, "x", axis=0, tiled=True)
        return own, swap(own, "c")

    def halves(values):
        width = values.shape[1] // 2
        return (
            lax.dynamic_slice(values, (0, c * width), (values.shape[0], width)),
            lax.dynamic_slice(values, (0, (1 - c) * width), (values.shape[0], width)),
        )

    out_own, out_other = gather_columns(after(w_out, pair))
    w_in = after(w_in, pieces[1])
    qkv_own, qkv_other = gather_columns(w_late)

    in_blocks = []
    for j in range(4):
        part = lax.dynamic_slice(w_in, (0, ((x + j) % 4) * 1024 + c * 512), (256, 512))
        in_blocks.append(part if j == 0 else shift(part, "x", j))
    fin_slice = lax.dynamic_slice(w_fin, (c * 512, 0), (512, 1024))
    bias_slice = lax.dynamic_slice(bias_in, (c * 512,), (512,)).astype(F32)

    bias_head = jnp.concatenate(
        [
            lax.dynamic_slice(full_bq, (head * 64,), (64,)),
            jnp.zeros((64,), F32),
            lax.dynamic_slice(full_bv, (head * 64,), (64,)),
            jnp.zeros((64,), F32),
        ]
    ).reshape(1, 256)
    q_wide, k_wide, v_wide, attf, att_blocks = attend(place, pieces, head_blocks, bias_head)
    *in_blocks, _ = lax.optimization_barrier(tuple(in_blocks) + (att_blocks,))
    in_blocks = [in_blocks[0], in_blocks[3], in_blocks[2], in_blocks[1]]
    in_slice = order_blocks(where, in_blocks)
    attended = (
        lax.all_to_all(att_blocks, SEQ_AXES, split_axis=0, concat_axis=0, tiled=True)
        .transpose(1, 0, 2)
        .reshape(128, 1024)
    )

    attended = after(attended, qkv_own)
    branch_own, branch_other = dot(attended, out_own), dot(attended, out_other)
    branch = jnp.where(
        c == 0,
        jnp.concatenate([branch_own, branch_other], 1),
        jnp.concatenate([branch_other, branch_own], 1),
    )
    first_sum = tokens.astype(F32) + branch + full_bo
    normed_one, factor_one = norm_parts(first_sum)
    first_norm = normed_one * full_g1 + full_s1
    norm_low = first_norm.astype(BF16)

    def gather_rows(own):
        parts = fetch_all(own, "x")
        return jnp.concatenate(parts + [swap(part, "c") for part in parts], 0)

    def scatter_rows(terms):
        own = terms[:512] + swap(terms[512:].astype(BF16), "c").astype(F32)
        own = lax.optimization_barrier(own)
        total = own[:128]
        for j in (2, 1, 3):
            block = own[128 * j : 128 * j + 128].astype(BF16)
            total = total + shift(block, "x", j).astype(F32)
        return total, own

    norm_rows = gather_rows(norm_low)
    pre_act = dot(norm_rows, in_slice) + bias_slice
    activated = jax.nn.gelu(pre_act, approximate=False).astype(BF16)
    ffn_out, _ = scatter_rows(dot(activated, fin_slice))
    second_sum = first_norm + ffn_out + full_bf
    normed_two, factor_two = norm_parts(second_sum)
    layer_out = (normed_two * full_g2 + full_s2).astype(BF16)
    grad_out = cotangent.astype(F32)
    d_gain_two = jnp.sum(grad_out * normed_two, 0)
    d_shift_two = jnp.sum(grad_out, 0)
    d_second = norm_back(grad_out * full_g2, normed_two, factor_two)
    d_second_low = d_second.astype(BF16)
    d_b_fin = column_sum(d_second_low)
    d_second_low = after(d_second_low, qkv_other)
    d_second_rows = gather_rows(d_second_low)
    d_pre = (times_trans(d_second_rows, fin_slice) * gelu_slope(pre_act)).astype(BF16)
    d_norm, pair_sum = scatter_rows(times_trans(d_pre, in_slice))
    activated, norm_rows, d_pre = lax.optimization_barrier(
        (activated, norm_rows, d_pre, pair_sum)
    )[:3]
    d_w_fin = outer_sum(activated, d_second_rows).astype(BF16)
    d_w_in = outer_sum(norm_rows, d_pre).astype(BF16)
    fin_terms = d_w_fin.reshape(16, 32, 1024)
    in_terms = d_w_in.reshape(4, 16, 16, 512).transpose(1, 0, 2, 3).reshape(16, 64, 512)
    fin_sum = plane_sum(fin_terms)
    d_norm = after(d_norm, fin_terms, in_terms)
    d_b_in = column_sum(d_pre)
    d_first_norm = d_norm + d_second
    d_gain_one = jnp.sum(d_first_norm * normed_one, 0)
    d_shift_one = jnp.sum(d_first_norm, 0)
    d_first = norm_back(d_first_norm * full_g1, normed_one, factor_one)
    d_first_low = d_first.astype(BF16)
    d_first_low = after(d_first_low, fin_sum)
    low_own, low_other = halves(d_first_low)
    d_attended = (times_trans(low_own, out_own) + times_trans(low_other, out_other)).astype(BF16)
    attended, d_first_low = lax.optimization_barrier((attended, d_first_low, d_attended))[:2]
    d_w_out = outer_sum(attended, d_first_low).astype(BF16)
    d_b_out = column_sum(d_first_low)
    d_blocks = lax.all_to_all(
        d_attended.reshape(128, 16, 64).transpose(1, 0, 2),
        SEQ_AXES,
        split_axis=0,
        concat_axis=0,
        tiled=True,
    )

    vec = jnp.stack([d_b_out, d_gain_one, d_shift_one, d_b_fin, d_gain_two, d_shift_two])
    vec = vec.astype(BF16).reshape(6, 4, 2, 128).transpose(2, 1, 0, 3)
    vec = jnp.pad(vec.reshape(2, 4, 1, 768), ((0, 0), (0, 0), (0, 15), (0, 256)))
    d_w_out = d_w_out.reshape(4, 2, 128, 1024)

    def core_terms(core):
        return (
            lax.dynamic_index_in_dim(d_w_out, core, 1, False),
            lax.dynamic_index_in_dim(vec, core, 0, False),
        )

    sent = swap(jnp.concatenate(core_terms(1 - c), 1), "c").astype(F32)
    out_own, vec_own = core_terms(c)
    out_pair = (out_own.astype(F32) + sent[:, :128]).astype(BF16)
    vec_pair = (vec_own.astype(F32) + sent[:, 128:]).astype(BF16)
    out_rows = out_pair.reshape(4, 16, 8, 2, 512).transpose(1, 0, 3, 2, 4)
    vec_rows = vec_pair[:, 0, :768].reshape(4, 16, 48).transpose(1, 0, 2)
    vec_rows = jnp.concatenate(
        [
            jnp.pad(vec_rows, ((0, 0), (0, 0), (0, 464))),
            jnp.pad(d_b_in.astype(BF16).reshape(16, 1, 32), ((0, 0), (0, 11), (0, 480))),
        ],
        1,
    )
    terms = jnp.concatenate([in_terms, out_rows.reshape(16, 64, 512), vec_rows], 1)
    fin_column = jnp.concatenate([fin_sum[:, :512], fin_sum[:, 512:]], 0)
    fin_column = jnp.stack(fetch_all(fin_column, Z_AXES))
    terms, d_blocks, fin_column = lax.optimization_barrier((terms, d_blocks, fin_column))
    fin_parts = fetch_all(fin_column, Y_AXES)
    summed = plane_sum(terms)
    d_abs, d_head = attend_back(place, q_wide, k_wide, v_wide, attf, d_blocks, pieces)

    summed = after(summed, d_abs)
    d_head = after(d_head, summed)
    *fin_parts, summed = lax.optimization_barrier(tuple(fin_parts) + (summed,))
    blocks = jnp.concatenate(
        [
            summed[:64].reshape(4, 16, 512),
            summed[64:128].reshape(4, 16, 512),
            jnp.pad(summed[128:132].reshape(4, 1, 512), ((0, 0), (0, 15), (0, 0))),
        ],
        1,
    )
    blocks = [lax.dynamic_index_in_dim(blocks, (x + j) % 4, 0, False) for j in range(4)]
    blocks = [blocks[0]] + [shift(blocks[j], "x", j) for j in (1, 2, 3)]
    total = sum(block[16:33].astype(F32) for block in blocks).astype(BF16)
    vec_row = jnp.concatenate([total[16:17, :48], summed[132:133, :32]], 1)
    plane = jnp.concatenate(
        [block[:16] for block in blocks]
        + [
            total[:16],
            jnp.pad(vec_row, ((0, 15), (0, 432))),
        ],
        0,
    )
    plane_row = jnp.stack(fetch_all(plane, Y_AXES))
    plane_parts = fetch_all(plane_row, Z_AXES)

    d_head = lax.all_to_all(d_head, ("x", "zh"), split_axis=0, concat_axis=0, tiled=True)
    fin_parts = fin_parts + [swap(part, "c") for part in fin_parts]
    (g_w_fin,) = lay(lay_fin_kernel, where, fin_parts, [(1024, 1024)], "lay_fin")
    d_head = after(d_head, plane, g_w_fin)
    d_head = jnp.sum(d_head.astype(F32), 0).astype(BF16)
    copies = lax.optimization_barrier(jnp.broadcast_to(d_head, (16, 208, 128)))
    heads = lax.all_to_all(copies, PLANE_AXES, split_axis=0, concat_axis=0, tiled=True)
    d_abs = after(d_abs, d_head, plane_row)
    d_back = lax.all_to_all(d_abs, SEQ_AXES, split_axis=0, concat_axis=0, tiled=True)
    g_w_qkv, g_b_qkv = lay(
        lay_qkv_kernel,
        where,
        [heads, swap(heads, "c")],
        [(256, 3072), (1, 3072)],
        "lay_qkv",
    )
    d_back = after(d_back, g_w_qkv)
    d_projected = d_back.reshape(16, 128, 3, 64).transpose(1, 2, 0, 3).reshape(128, 3072)
    proj_own, proj_other = halves(d_projected)
    grad_tokens = times_trans(proj_own, qkv_own) + times_trans(proj_other, qkv_other) + d_first

    plane_parts = plane_parts + [swap(part, "c") for part in plane_parts]
    g_w_in, g_w_out, g_vec = lay(
        lay_ffn_kernel,
        where,
        plane_parts,
        [(256, 4096), (256, 1024), (32, 8, 128)],
        "lay_ffn",
    )
    g_vec = g_vec[:, 0, :80]
    g_six = g_vec[:, :48].reshape(2, 6, 128).transpose(1, 0, 2).reshape(6, 256)
    g_b_in = g_vec[:, 48:].reshape(1024)
    g_b_q = lax.dynamic_slice(g_b_qkv[0], (x * 256,), (256,))
    g_b_v = lax.dynamic_slice(g_b_qkv[0], (2048 + x * 256,), (256,))
    return (
        layer_out,
        grad_tokens,
        g_w_qkv,
        g_b_q,
        g_b_v,
        g_w_out,
        g_six[0],
        g_six[1],
        g_six[2],
        g_w_in,
        g_b_in,
        g_w_fin,
        g_six[3],
        g_six[4],
        g_six[5],
    )


def solution(mesh):
    fine = Mesh(mesh.devices.reshape(SIZES), AXES)
    rows = P(AXES, None)
    matrix = P("x", None)
    vector = P("x")
    in_specs = (
        rows,
        matrix,
        vector,
        vector,
        matrix,
        vector,
        vector,
        vector,
        matrix,
        vector,
        matrix,
        vector,
        vector,
        vector,
        rows,
    )
    out_specs = (
        rows,
        rows,
        matrix,
        vector,
        vector,
        matrix,
        vector,
        vector,
        vector,
        matrix,
        vector,
        matrix,
        vector,
        vector,
        vector,
    )
    return jax.shard_map(shards, mesh=fine, in_specs=in_specs, out_specs=out_specs, check_vma=False)
```

```python
import functools
import math

import jax
import jax.numpy as jnp
from jax import lax
from jax.experimental import pallas as pl
from jax.experimental.pallas import tpu as pltpu
from jax.sharding import Mesh, PartitionSpec as P

AXES = ("x", "zh", "zl", "yl", "c", "yh")
SIZES = (4, 2, 2, 2, 2, 2)
SEQ_AXES = ("zl", "yl", "c", "yh")
Y_AXES = ("yl", "yh")
Z_AXES = ("zh", "zl")
PLANE_AXES = ("zh", "zl", "yl", "yh")
D = 1024
FF = 4096
HEAD_DIM = 64
F32 = jnp.float32
BF16 = jnp.bfloat16

norm_eps = 1e-12
inv_root_two = 1.0 / math.sqrt(2.0)
inv_root_tau = 1.0 / math.sqrt(2.0 * math.pi)


def y_slot(y):
    return (y % 2) * 2 + y // 2


def shift(value, axis, step):
    slot = y_slot if axis == Y_AXES else (lambda i: i)
    return lax.ppermute(value, axis, [(slot(i), slot((i + step) % 4)) for i in range(4)])


def swap(value, axis):
    return lax.ppermute(value, axis, [(0, 1), (1, 0)])


def fetch_all(value, axis):
    return [value] + [shift(value, axis, -j) for j in (1, 2, 3)]


def after(value, *others):
    return lax.optimization_barrier((value,) + others)[0]


def roll_blocks(blocks, me):
    twice = jnp.stack(blocks + blocks)
    return lax.dynamic_slice_in_dim(twice, (4 - me) % 4, 4, 0)


def dot(left_op, right_op):
    return jnp.dot(left_op, right_op, preferred_element_type=F32)


def outer_sum(left_op, right_op):
    return lax.dot_general(left_op, right_op, (((0,), (0,)), ((), ())), preferred_element_type=F32)


def times_trans(left_op, right_op):
    return lax.dot_general(left_op, right_op, (((1,), (1,)), ((), ())), preferred_element_type=F32)


def norm_parts(summed):
    row_mean = jnp.mean(summed, -1, keepdims=True)
    centered = summed - row_mean
    factor = lax.rsqrt(jnp.mean(centered * centered, -1, keepdims=True) + norm_eps)
    return (centered * factor, factor)


def norm_back(scaled_grad, normed, factor):
    return factor * (
        scaled_grad
        - jnp.mean(scaled_grad, -1, keepdims=True)
        - normed * jnp.mean(scaled_grad * normed, -1, keepdims=True)
    )


def gelu_slope(pre_act):
    return (
        0.5 * (1.0 + lax.erf(pre_act * inv_root_two))
        + pre_act * jnp.exp(-0.5 * pre_act * pre_act) * inv_root_tau
    )


def column_sum(values):
    return jnp.sum(values.astype(F32), 0)


def three_terms(column):
    high = column.astype(BF16).astype(F32)
    rest = column - high
    middle = rest.astype(BF16).astype(F32)
    return high, middle, rest - middle


def widen(values, column):
    rows = values.shape[0]
    lane = lax.broadcasted_iota(jnp.int32, (rows, HEAD_DIM), 1)
    high, middle, low = three_terms(-column)
    extra = jnp.where(lane == 0, high, jnp.where(lane == 1, middle, jnp.where(lane == 2, low, 0.0)))
    return jnp.concatenate([values.astype(F32), extra], 1).astype(BF16)


def with_ones(values):
    rows = values.shape[0]
    lane = lax.broadcasted_iota(jnp.int32, (rows, HEAD_DIM), 1)
    return jnp.concatenate([values.astype(F32), jnp.where(lane < 3, 1.0, 0.0)], 1).astype(BF16)


PIECE_ROWS = (256,) * 8


def attend_kernel(place, *refs):
    pieces = refs[:8]
    blocks = refs[8:12]
    bias, q_out, k_out, v_out, attf_out, att_out, weight = refs[12:]
    for j in range(4):
        weight[(place[16] + j) % 4] = blocks[j][...]
    whole = weight[...].reshape(1024, 256)
    start = 0
    for piece, count in zip(pieces, PIECE_ROWS):
        proj = dot(piece[...], whole) + bias[...]
        rows = pl.ds(start, count)
        query = proj[:, :64].astype(BF16).astype(F32) * 0.125
        q_out[rows, :] = jnp.concatenate([query, jnp.zeros_like(query)], 1).astype(BF16)
        k_out[rows, :] = with_ones(proj[:, 64:128])
        v_out[rows, :] = with_ones(proj[:, 128:192])
        start += count

    @pl.loop(0, 8, unroll=2)
    def _(i):
        rows = pl.ds(pl.multiple_of(256 * i, 256), 256)
        query = q_out[rows, :]
        scores = times_trans(query, k_out[...])
        top = jnp.max(scores, 1, keepdims=True)
        probs = jnp.exp(scores - top).astype(BF16)
        weighted = dot(probs, v_out[...])
        total = weighted[:, 64:65]
        attended = weighted[:, :64] / total
        q_out[rows, :] = widen(query[:, :64], top + jnp.log(total))
        attf_out[rows, :] = attended
        low = attended.astype(BF16)
        att_out[place[2 * i]] = low[:128]
        att_out[place[2 * i + 1]] = low[128:]


def attend(place, pieces, blocks, bias):
    vmem = pl.BlockSpec(memory_space=pltpu.VMEM)
    wide = jax.ShapeDtypeStruct((2048, 128), BF16)
    return pl.pallas_call(
        attend_kernel,
        in_specs=[pl.BlockSpec(memory_space=pltpu.SMEM)] + [vmem] * 13,
        out_specs=[vmem] * 5,
        out_shape=[
            wide,
            wide,
            wide,
            jax.ShapeDtypeStruct((2048, 64), F32),
            jax.ShapeDtypeStruct((16, 128, 64), BF16),
        ],
        scratch_shapes=[pltpu.VMEM((4, 256, 256), BF16)],
        compiler_params=pltpu.CompilerParams(vmem_limit_bytes=24 * 2**20),
        cost_estimate=pl.CostEstimate(flops=3 * 10**9, bytes_accessed=6 * 10**6, transcendentals=2**22),
        name="attend",
    )(place, *pieces, *blocks, bias)


def attend_back_kernel(place, q_ref, k_ref, v_ref, attf, dout, *refs):
    pieces = refs[:8]
    abs_out, head_out, g_wide, dq_acc, rel, held, arrived = refs[8:]
    copies = [pltpu.make_async_copy(pieces[i], held.at[i], arrived.at[i]) for i in range(8)]
    for copy in copies:
        copy.start()
    for r in range(16):
        rows = pl.ds(128 * r, 128)
        grad = dout[place[r]]
        delta = jnp.sum(grad.astype(F32) * attf[rows, :], 1, keepdims=True)
        g_wide[rows, :] = widen(grad, delta)
    dq_acc[...] = jnp.zeros_like(dq_acc)

    @pl.loop(0, 8, unroll=2)
    def _(j):
        rows = pl.ds(pl.multiple_of(256 * j, 256), 256)
        keys = k_ref[rows, :]
        probs = jnp.exp(times_trans(keys, q_ref[...]))
        d_less = times_trans(v_ref[rows, :], g_wide[...])
        d_scores = (probs * d_less).astype(BF16)
        d_val = dot(probs.astype(BF16), g_wide[...])[:, :64]
        d_key = dot(d_scores, q_ref[...])[:, :64]
        dq_acc[...] += outer_sum(keys, d_scores)
        rel[rows, :] = jnp.concatenate([jnp.zeros_like(d_key), d_key, d_val], 1).astype(BF16)

    sums = jnp.zeros((1, 192), F32)
    d_queries = (dq_acc[:64, :] * 0.125).T
    for r in range(16):
        rows = pl.ds(128 * r, 128)
        d_query = d_queries[128 * r : 128 * r + 128].astype(BF16)
        both = jnp.concatenate([d_query, rel[rows, :][:, 64:192]], 1)
        rel[rows, :] = both
        abs_out[place[r]] = both
        sums = sums + jnp.sum(both.astype(F32), 0, keepdims=True)

    grad = jnp.zeros((192, 1024), F32)
    for i in range(8):
        copies[i].wait()
        grad = grad + outer_sum(rel[256 * i : 256 * i + 256, :], held[i])
    grad = grad.T
    row = lax.broadcasted_iota(jnp.int32, (16, 128), 0)
    tail = jnp.where(
        row == 0,
        sums[:, :128],
        jnp.where(
            row == 1, jnp.concatenate([sums[:, 128:], jnp.zeros((1, 64), F32)], 1), 0.0
        ),
    ).astype(BF16)
    for owner in range(8):
        rows = grad[128 * owner : 128 * owner + 128]
        for part in range(3):
            cols = rows[:, 64 * part : 64 * part + 64]
            head_out[owner, 64 * part : 64 * part + 64, :] = jnp.concatenate(
                [cols[:64], cols[64:]], 1
            ).astype(BF16)
        head_out[owner, 192:208, :] = tail


def attend_back(place, q_wide, k_wide, v_wide, attf, dout, pieces):
    vmem = pl.BlockSpec(memory_space=pltpu.VMEM)
    return pl.pallas_call(
        attend_back_kernel,
        in_specs=[pl.BlockSpec(memory_space=pltpu.SMEM)]
        + [vmem] * 5
        + [pl.BlockSpec(memory_space=pl.ANY)] * 8,
        out_specs=[vmem] * 2,
        out_shape=[
            jax.ShapeDtypeStruct((16, 128, 192), BF16),
            jax.ShapeDtypeStruct((8, 208, 128), BF16),
        ],
        scratch_shapes=[
            pltpu.VMEM((2048, 128), BF16),
            pltpu.VMEM((128, 2048), F32),
            pltpu.VMEM((2048, 192), BF16),
            pltpu.VMEM((8, 256, 1024), BF16),
            pltpu.SemaphoreType.DMA((8,)),
        ],
        compiler_params=pltpu.CompilerParams(vmem_limit_bytes=40 * 2**20),
        cost_estimate=pl.CostEstimate(flops=10**10, bytes_accessed=8 * 10**6, transcendentals=2**22),
        name="attend_back",
    )(place, q_wide, k_wide, v_wide, attf, dout, *pieces)


def chip_row(y, z):
    return z * 4 + y_slot(y)


def lay_fin_kernel(where, *refs):
    grads, out = refs[:8], refs[8]
    y, z, c = where[1], where[2], where[3]
    for cj in range(2):
        core = (c + cj) % 2
        for yj in range(4):
            for zj in range(4):
                chip = chip_row((y + yj) % 4, (z + zj) % 4)
                for half in range(2):
                    out[
                        pl.ds(pl.multiple_of(core * 512 + chip * 32, 32), 32),
                        512 * half : 512 * half + 512,
                    ] = grads[cj * 4 + yj][zj, 32 * half : 32 * half + 32].astype(F32)


def lay_ffn_kernel(where, *refs):
    grads = refs[:8]
    win_out, wout_out, vec_out = refs[8:]
    x, y, z, c = where[0], where[1], where[2], where[3]
    for cj in range(2):
        core = (c + cj) % 2
        for yj in range(4):
            for zj in range(4):
                chip = chip_row((y + yj) % 4, (z + zj) % 4)
                piece = grads[cj * 4 + zj]
                for xj in range(4):
                    owner = (x + 4 - xj) % 4
                    col = pl.multiple_of(owner * 1024 + core * 512, 512)
                    win_out[pl.ds(pl.multiple_of(chip * 16, 16), 16), pl.ds(col, 512)] = piece[
                        yj, 16 * xj : 16 * xj + 16
                    ].astype(F32)
                rest = piece[yj, 64:96].astype(F32)
                for half in range(2):
                    wout_out[
                        pl.ds(pl.multiple_of(core * 128 + chip * 8, 8), 8),
                        512 * half : 512 * half + 512,
                    ] = rest[8 * half : 8 * half + 8]
                vec_out[core * 16 + chip] = rest[16:24, 0:128]


def lay_qkv_kernel(where, *refs):
    grads = refs[:2]
    w_out, b_out = refs[2:]
    c = where[3]
    for cj in range(2):
        core = (c + cj) % 2
        for zz in range(4):
            for yl in range(2):
                chip = zz * 4 + yl * 2
                low = grads[cj][chip].astype(F32)
                high = grads[cj][chip + 1].astype(F32)
                head = (zz % 2) * 8 + yl * 4 + core * 2
                base = (zz // 2) * 128
                for part in range(3):
                    rows = slice(part * 64, part * 64 + 64)
                    col = pl.multiple_of(part * 1024 + head * 64, 128)
                    for half in range(2):
                        lanes = slice(half * 64, half * 64 + 64)
                        w_out[
                            base + half * 64 : base + half * 64 + 64, pl.ds(col, 128)
                        ] = jnp.concatenate([low[rows, lanes], high[rows, lanes]], 1)
                    if part != 1:
                        row = 192 + part // 2
                        b_out[:, pl.ds(col, 128)] = jnp.concatenate(
                            [low[row : row + 1, :64], high[row : row + 1, :64]], 1
                        )


def lay(kernel, where, grads, shapes, name):
    count = len(grads)

    def body(where_ref, *refs):
        sources, outs = refs[:count], refs[count : count + len(shapes)]
        held, arrived = refs[count + len(shapes) : -1], refs[-1]
        copies = [pltpu.make_async_copy(sources[i], held[i], arrived.at[i]) for i in range(count)]
        for copy in copies:
            copy.start()
        for copy in copies:
            copy.wait()
        kernel(where_ref, *held, *outs)

    vmem = pl.BlockSpec(memory_space=pltpu.VMEM)
    return pl.pallas_call(
        body,
        in_specs=[pl.BlockSpec(memory_space=pltpu.SMEM)]
        + [pl.BlockSpec(memory_space=pl.ANY)] * count,
        out_specs=[vmem] * len(shapes),
        out_shape=[jax.ShapeDtypeStruct(s, F32) for s in shapes],
        scratch_shapes=[pltpu.VMEM(g.shape, BF16) for g in grads]
        + [pltpu.SemaphoreType.DMA((count,))],
        compiler_params=pltpu.CompilerParams(vmem_limit_bytes=24 * 2**20),
        cost_estimate=pl.CostEstimate(flops=10**6, bytes_accessed=15 * 10**6, transcendentals=0),
        name=name,
    )(where, *grads)


def plane_sum(terms):
    sent = lax.all_to_all(terms, PLANE_AXES, split_axis=0, concat_axis=0, tiled=True)
    return jnp.sum(sent.astype(F32), 0).astype(BF16)


def order_kernel(where, *refs):
    for j in range(4):
        refs[4][(where[0] + j) % 4] = refs[j][...]


def order_blocks(where, blocks):
    vmem = pl.BlockSpec(memory_space=pltpu.VMEM)
    rows, width = blocks[0].shape
    whole = pl.pallas_call(
        order_kernel,
        in_specs=[pl.BlockSpec(memory_space=pltpu.SMEM)] + [vmem] * 4,
        out_specs=vmem,
        out_shape=jax.ShapeDtypeStruct((4, rows, width), BF16),
        compiler_params=pltpu.CompilerParams(vmem_limit_bytes=24 * 2**20),
        name="order_blocks",
    )(where, *blocks)
    return whole.reshape(4 * rows, width)


def shards(
    tokens,
    w_qkv,
    bias_q,
    bias_v,
    w_out,
    bias_o,
    gain_attn,
    shift_attn,
    w_in,
    bias_in,
    w_fin,
    bias_fin,
    gain_ffn,
    shift_ffn,
    cotangent,
):
    x = lax.axis_index("x")
    zh = lax.axis_index("zh")
    zl = lax.axis_index("zl")
    yl = lax.axis_index("yl")
    c = lax.axis_index("c")
    yh = lax.axis_index("yh")
    y = yh * 2 + yl
    z = zh * 2 + zl
    head = zl * 8 + yl * 4 + c * 2 + yh
    where = jnp.stack([x, y, z, c]).astype(jnp.int32)
    places = []
    for cj in range(2):
        for yj in range(4):
            for zj in range(2):
                y_now = (y + yj) % 4
                places.append(((zl + zj) % 2) * 8 + (y_now % 2) * 4 + ((c + cj) % 2) * 2 + y_now // 2)
    place = jnp.stack(places + [x]).astype(jnp.int32)

    pair = jnp.concatenate([tokens, swap(tokens, "zl")], 0)
    mine = fetch_all(pair, Y_AXES)
    pieces = mine + [swap(part, "c") for part in mine]
    w_late = after(w_qkv, pair)
    vectors = jnp.stack(
        [bias_q, bias_v, bias_o, gain_attn, shift_attn, bias_fin, gain_ffn, shift_ffn], 1
    )
    head_cols = jnp.concatenate(
        [lax.dynamic_slice(w_late, (0, part * 1024 + head * 64), (256, 64)) for part in range(3)]
        + [vectors, jnp.zeros((256, 56), BF16)],
        1,
    )
    head_blocks = fetch_all(head_cols, "x")
    full = roll_blocks([block[:, 192:200] for block in head_blocks], x)
    full = full.reshape(1024, 8).T.astype(F32)
    full_bq, full_bv, full_bo, full_g1, full_s1, full_bf, full_g2, full_s2 = [
        full[i] for i in range(8)
    ]

    def gather_columns(weight):
        width = weight.shape[1] // 2
        own = lax.dynamic_slice(weight, (0, c * width), (256, width))
        own = lax.all_gather(own, "x", axis=0, tiled=True)
        return own, swap(own, "c")

    def halves(values):
        width = values.shape[1] // 2
        return (
            lax.dynamic_slice(values, (0, c * width), (values.shape[0], width)),
            lax.dynamic_slice(values, (0, (1 - c) * width), (values.shape[0], width)),
        )

    out_own, out_other = gather_columns(after(w_out, pair))
    w_in = after(w_in, pieces[1])
    qkv_own, qkv_other = gather_columns(w_late)

    in_blocks = []
    for j in range(4):
        part = lax.dynamic_slice(w_in, (0, ((x + j) % 4) * 1024 + c * 512), (256, 512))
        in_blocks.append(part if j == 0 else shift(part, "x", j))
    fin_slice = lax.dynamic_slice(w_fin, (c * 512, 0), (512, 1024))
    bias_slice = lax.dynamic_slice(bias_in, (c * 512,), (512,)).astype(F32)

    bias_head = jnp.concatenate(
        [
            lax.dynamic_slice(full_bq, (head * 64,), (64,)),
            jnp.zeros((64,), F32),
            lax.dynamic_slice(full_bv, (head * 64,), (64,)),
            jnp.zeros((64,), F32),
        ]
    ).reshape(1, 256)
    q_wide, k_wide, v_wide, attf, att_blocks = attend(place, pieces, head_blocks, bias_head)
    *in_blocks, _ = lax.optimization_barrier(tuple(in_blocks) + (att_blocks,))
    in_blocks = [in_blocks[0], in_blocks[3], in_blocks[2], in_blocks[1]]
    in_slice = order_blocks(where, in_blocks)
    attended = (
        lax.all_to_all(att_blocks, SEQ_AXES, split_axis=0, concat_axis=0, tiled=True)
        .transpose(1, 0, 2)
        .reshape(128, 1024)
    )

    attended = after(attended, qkv_own)
    branch_own, branch_other = dot(attended, out_own), dot(attended, out_other)
    branch = jnp.where(
        c == 0,
        jnp.concatenate([branch_own, branch_other], 1),
        jnp.concatenate([branch_other, branch_own], 1),
    )
    first_sum = tokens.astype(F32) + branch + full_bo
    normed_one, factor_one = norm_parts(first_sum)
    first_norm = normed_one * full_g1 + full_s1
    norm_low = first_norm.astype(BF16)

    def gather_rows(own):
        parts = fetch_all(own, "x")
        return jnp.concatenate(parts + [swap(part, "c") for part in parts], 0)

    def scatter_rows(terms):
        own = terms[:512] + swap(terms[512:].astype(BF16), "c").astype(F32)
        own = lax.optimization_barrier(own)
        total = own[:128]
        for j in (2, 1, 3):
            block = own[128 * j : 128 * j + 128].astype(BF16)
            total = total + shift(block, "x", j).astype(F32)
        return total, own

    norm_rows = gather_rows(norm_low)
    pre_act = dot(norm_rows, in_slice) + bias_slice
    activated = jax.nn.gelu(pre_act, approximate=False).astype(BF16)
    ffn_out, _ = scatter_rows(dot(activated, fin_slice))
    second_sum = first_norm + ffn_out + full_bf
    normed_two, factor_two = norm_parts(second_sum)
    layer_out = (normed_two * full_g2 + full_s2).astype(BF16)
    grad_out = cotangent.astype(F32)
    d_gain_two = jnp.sum(grad_out * normed_two, 0)
    d_shift_two = jnp.sum(grad_out, 0)
    d_second = norm_back(grad_out * full_g2, normed_two, factor_two)
    d_second_low = d_second.astype(BF16)
    d_b_fin = column_sum(d_second_low)
    d_second_low = after(d_second_low, qkv_other)
    d_second_rows = gather_rows(d_second_low)
    d_pre = (times_trans(d_second_rows, fin_slice) * gelu_slope(pre_act)).astype(BF16)
    d_norm, pair_sum = scatter_rows(times_trans(d_pre, in_slice))
    activated, norm_rows, d_pre = lax.optimization_barrier(
        (activated, norm_rows, d_pre, pair_sum)
    )[:3]
    d_w_fin = outer_sum(activated, d_second_rows).astype(BF16)
    d_w_in = outer_sum(norm_rows, d_pre).astype(BF16)
    fin_terms = d_w_fin.reshape(16, 32, 1024)
    in_terms = d_w_in.reshape(4, 16, 16, 512).transpose(1, 0, 2, 3).reshape(16, 64, 512)
    fin_sum = plane_sum(fin_terms)
    d_norm = after(d_norm, fin_terms, in_terms)
    d_b_in = column_sum(d_pre)
    d_first_norm = d_norm + d_second
    d_gain_one = jnp.sum(d_first_norm * normed_one, 0)
    d_shift_one = jnp.sum(d_first_norm, 0)
    d_first = norm_back(d_first_norm * full_g1, normed_one, factor_one)
    d_first_low = d_first.astype(BF16)
    d_first_low = after(d_first_low, fin_sum)
    low_own, low_other = halves(d_first_low)
    d_attended = (times_trans(low_own, out_own) + times_trans(low_other, out_other)).astype(BF16)
    attended, d_first_low = lax.optimization_barrier((attended, d_first_low, d_attended))[:2]
    d_w_out = outer_sum(attended, d_first_low).astype(BF16)
    d_b_out = column_sum(d_first_low)
    d_blocks = lax.all_to_all(
        d_attended.reshape(128, 16, 64).transpose(1, 0, 2),
        SEQ_AXES,
        split_axis=0,
        concat_axis=0,
        tiled=True,
    )

    vec = jnp.stack([d_b_out, d_gain_one, d_shift_one, d_b_fin, d_gain_two, d_shift_two])
    vec = vec.astype(BF16).reshape(6, 4, 2, 128).transpose(2, 1, 0, 3)
    vec = jnp.pad(vec.reshape(2, 4, 1, 768), ((0, 0), (0, 0), (0, 15), (0, 256)))
    d_w_out = d_w_out.reshape(4, 2, 128, 1024)

    def core_terms(core):
        return (
            lax.dynamic_index_in_dim(d_w_out, core, 1, False),
            lax.dynamic_index_in_dim(vec, core, 0, False),
        )

    sent = swap(jnp.concatenate(core_terms(1 - c), 1), "c").astype(F32)
    out_own, vec_own = core_terms(c)
    out_pair = (out_own.astype(F32) + sent[:, :128]).astype(BF16)
    vec_pair = (vec_own.astype(F32) + sent[:, 128:]).astype(BF16)
    out_rows = out_pair.reshape(4, 16, 8, 2, 512).transpose(1, 0, 3, 2, 4)
    vec_rows = vec_pair[:, 0, :768].reshape(4, 16, 48).transpose(1, 0, 2)
    vec_rows = jnp.concatenate(
        [
            jnp.pad(vec_rows, ((0, 0), (0, 0), (0, 464))),
            jnp.pad(d_b_in.astype(BF16).reshape(16, 1, 32), ((0, 0), (0, 11), (0, 480))),
        ],
        1,
    )
    terms = jnp.concatenate([in_terms, out_rows.reshape(16, 64, 512), vec_rows], 1)
    fin_column = jnp.concatenate([fin_sum[:, :512], fin_sum[:, 512:]], 0)
    fin_column = jnp.stack(fetch_all(fin_column, Z_AXES))
    terms, d_blocks, fin_column = lax.optimization_barrier((terms, d_blocks, fin_column))
    fin_parts = fetch_all(fin_column, Y_AXES)
    summed = plane_sum(terms)
    d_abs, d_head = attend_back(place, q_wide, k_wide, v_wide, attf, d_blocks, pieces)

    summed = after(summed, d_abs)
    d_head = after(d_head, summed)
    *fin_parts, summed = lax.optimization_barrier(tuple(fin_parts) + (summed,))
    blocks = jnp.concatenate(
        [
            summed[:64].reshape(4, 16, 512),
            summed[64:128].reshape(4, 16, 512),
            jnp.pad(summed[128:132].reshape(4, 1, 512), ((0, 0), (0, 15), (0, 0))),
        ],
        1,
    )
    blocks = [lax.dynamic_index_in_dim(blocks, (x + j) % 4, 0, False) for j in range(4)]
    blocks = [blocks[0]] + [shift(blocks[j], "x", j) for j in (1, 2, 3)]
    total = sum(block[16:33].astype(F32) for block in blocks).astype(BF16)
    vec_row = jnp.concatenate([total[16:17, :48], summed[132:133, :32]], 1)
    plane = jnp.concatenate(
        [block[:16] for block in blocks]
        + [
            total[:16],
            jnp.pad(vec_row, ((0, 15), (0, 432))),
        ],
        0,
    )
    plane_row = jnp.stack(fetch_all(plane, Y_AXES))
    plane_parts = fetch_all(plane_row, Z_AXES)

    d_head = lax.all_to_all(d_head, ("x", "zh"), split_axis=0, concat_axis=0, tiled=True)
    fin_parts = fin_parts + [swap(part, "c") for part in fin_parts]
    (g_w_fin,) = lay(lay_fin_kernel, where, fin_parts, [(1024, 1024)], "lay_fin")
    d_head = after(d_head, plane, g_w_fin)
    d_head = jnp.sum(d_head.astype(F32), 0).astype(BF16)
    copies = lax.optimization_barrier(jnp.broadcast_to(d_head, (16, 208, 128)))
    heads = lax.all_to_all(copies, PLANE_AXES, split_axis=0, concat_axis=0, tiled=True)
    d_abs = after(d_abs, heads)
    d_back = lax.all_to_all(d_abs, SEQ_AXES, split_axis=0, concat_axis=0, tiled=True)
    g_w_qkv, g_b_qkv = lay(
        lay_qkv_kernel,
        where,
        [heads, swap(heads, "c")],
        [(256, 3072), (1, 3072)],
        "lay_qkv",
    )
    d_back = after(d_back, g_w_qkv)
    d_projected = d_back.reshape(16, 128, 3, 64).transpose(1, 2, 0, 3).reshape(128, 3072)
    proj_own, proj_other = halves(d_projected)
    grad_tokens = times_trans(proj_own, qkv_own) + times_trans(proj_other, qkv_other) + d_first

    plane_parts = plane_parts + [swap(part, "c") for part in plane_parts]
    g_w_in, g_w_out, g_vec = lay(
        lay_ffn_kernel,
        where,
        plane_parts,
        [(256, 4096), (256, 1024), (32, 8, 128)],
        "lay_ffn",
    )
    g_vec = g_vec[:, 0, :80]
    g_six = g_vec[:, :48].reshape(2, 6, 128).transpose(1, 0, 2).reshape(6, 256)
    g_b_in = g_vec[:, 48:].reshape(1024)
    g_b_q = lax.dynamic_slice(g_b_qkv[0], (x * 256,), (256,))
    g_b_v = lax.dynamic_slice(g_b_qkv[0], (2048 + x * 256,), (256,))
    return (
        layer_out,
        grad_tokens,
        g_w_qkv,
        g_b_q,
        g_b_v,
        g_w_out,
        g_six[0],
        g_six[1],
        g_six[2],
        g_w_in,
        g_b_in,
        g_w_fin,
        g_six[3],
        g_six[4],
        g_six[5],
    )


def solution(mesh):
    fine = Mesh(mesh.devices.reshape(SIZES), AXES)
    rows = P(AXES, None)
    matrix = P("x", None)
    vector = P("x")
    in_specs = (
        rows,
        matrix,
        vector,
        vector,
        matrix,
        vector,
        vector,
        vector,
        matrix,
        vector,
        matrix,
        vector,
        vector,
        vector,
        rows,
    )
    out_specs = (
        rows,
        rows,
        matrix,
        vector,
        vector,
        matrix,
        vector,
        vector,
        vector,
        matrix,
        vector,
        matrix,
        vector,
        vector,
        vector,
    )
    return jax.shard_map(shards, mesh=fine, in_specs=in_specs, out_specs=out_specs, check_vma=False)
```
